32 devices in a mesh: rep: 16 (over z, x, core), shard: 2 (over y).
Axes of the slice: x: 2, y: 2, z: 4, core: 2. Of those that a mesh axis runs over, the one named last changes fastest.
Arguments:
- inputs: bfloat16 [32, 512, 768], P('rep', 'shard'), may hold values from -6 to 6
- doc_lengths: int32 [32, 4], P('rep'), may hold values from 1 to 509, as said below
- qkv_weight: bfloat16 [768, 2304], P('shard'), may hold values from -0.3125 to 0.3125
- qv_bias: bfloat16 [1536], P('shard'), may hold values from -1.796875 to 1.796875
- out_weight: bfloat16 [768, 768], P('shard'), may hold values from -1.25 to 1.25
- out_bias: bfloat16 [768], P('shard'), may hold values from -1.796875 to 1.796875
- first_gain: bfloat16 [768], P('shard'), may hold values from 0.5 to 1.5
- first_shift: bfloat16 [768], P('shard'), may hold values from -1.796875 to 1.796875
- up_weight: bfloat16 [768, 3072], P('shard'), may hold values from -0.21875 to 0.21875
- up_bias: bfloat16 [3072], P('shard'), may hold values from -1.796875 to 1.796875
- down_weight: bfloat16 [3072, 768], P('shard'), may hold values from -0.15625 to 0.15625
- down_bias: bfloat16 [768], P('shard'), may hold values from -1.796875 to 1.796875
- second_gain: bfloat16 [768], P('shard'), may hold values from 0.5 to 1.5
- second_shift: bfloat16 [768], P('shard'), may hold values from -1.796875 to 1.796875
- grad_out: bfloat16 [32, 512, 768], P('rep', 'shard'), may hold values from -6 to 6
Outputs:
- layer_out: bfloat16 [32, 512, 768], P('rep', 'shard')
- input_grad: float32 [32, 512, 768], P('rep', 'shard')
- qkv_weight_grad: float32 [768, 2304], P('shard')
- qv_bias_grad: float32 [1536], P('shard')
- out_weight_grad: float32 [768, 768], P('shard')
- out_bias_grad: float32 [768], P('shard')
- first_gain_grad: float32 [768], P('shard')
- first_shift_grad: float32 [768], P('shard')
- up_weight_grad: float32 [768, 3072], P('shard')
- up_bias_grad: float32 [3072], P('shard')
- down_weight_grad: float32 [3072, 768], P('shard')
- down_bias_grad: float32 [768], P('shard')
- second_gain_grad: float32 [768], P('shard')
- second_shift_grad: float32 [768], P('shard')
The draws below stay inside these ranges and needn't reach their ends.
Inputs may be any that keep to these rules, and one draw needn't show every extreme that they name: `doc_lengths`: each row lists in order the lengths of the 4 documents packed into one sequence; a row sums to 512.
All inputs are finite; a program needn't handle non-finite values.
Results may differ from the reference program's by a relative error of at most 0.014.
The reference program's roundings to bfloat16 on the way count: a program that leaves them out, or rounds other values in their place, can miss the bound.
Values may be sent and summed in bfloat16 or wider, within the bound.
A program may use at most 192 MiB of HBM per device.

```python
import jax
import jax.numpy as jnp
from jax import lax

D = 768
HEADS = 12
HEAD_DIM = 64
FF = 3072
SEQ = 512
SEQS = 2
NDOCS = 4
BATCH = 32
N_REP = 16
N_SHARD = 2


def draw_doc_lengths(key, part):
    key = jax.random.fold_in(key, 7)
    rows_dev = SEQ // N_SHARD
    lead_key, tail_key, split_key, pick_key, group_key, cut_key = jax.random.split(key, 6)
    lead_len = jax.random.randint(lead_key, (BATCH,), 1, rows_dev)
    tail_len = jax.random.randint(tail_key, (BATCH,), 2, rows_dev)
    row_index = jnp.arange(BATCH, dtype=jnp.int32)
    group_index = row_index // SEQS
    slot_index = row_index % SEQS
    spanning_slot = jax.random.randint(group_key, (N_REP,), 0, SEQS)
    span_rows = slot_index == spanning_slot[group_index]
    marked_group = jax.random.randint(pick_key, (), 0, N_REP)
    marked = span_rows & (group_index == marked_group)
    lead_len = jnp.where(marked, 1, lead_len)
    tail_len = jnp.where(marked, 2, tail_len)
    third_len = jax.random.randint(split_key, (BATCH,), 1, tail_len)
    fourth_len = tail_len - third_len
    longest = SEQ - lead_len - tail_len
    spanning = jnp.stack([lead_len, longest, third_len, fourth_len], axis=1).astype(jnp.int32)

    def cut_row(row_key):
        chosen_points = jax.random.permutation(row_key, SEQ - 1)[:NDOCS - 1] + 1
        return jnp.sort(chosen_points)
    cut_points = jax.vmap(cut_row)(jax.random.split(cut_key, BATCH)).astype(jnp.int32)
    bounds = jnp.concatenate([jnp.zeros((BATCH, 1), jnp.int32), cut_points, jnp.full((BATCH, 1), SEQ, jnp.int32)], axis=1)
    spread_rows = bounds[:, 1:] - bounds[:, :-1]
    return jnp.where(span_rows[:, None], spanning, spread_rows).astype(jnp.int32)


def level_of(rng, shape, shards, least, top_value):
    factor_of = 1.0
    for position, shards_of in shards:
        heights = jax.random.uniform(jax.random.fold_in(jax.random.fold_in(rng, 6), position), (shards_of,), jnp.float32, least / len(shards), top_value / len(shards))
        factor_of = factor_of * jnp.repeat(jnp.exp(heights), shape[position] // shards_of).reshape((-1,) + (1,) * (len(shape) - 1 - position))
    return factor_of


def normal_values(rng, extent, deviation, reach, cuts=(), kind=jnp.bfloat16):
    entries = deviation * jax.random.normal(rng, extent, jnp.float32)
    if cuts:
        entries = entries * level_of(rng, extent, cuts, -0.22, 0.18)
    return jnp.clip(entries, -reach, reach).astype(kind)


def setup_inputs(seed: int = 0) -> dict:
    seeds = jax.random.split(jax.random.key(seed), 16)
    return {
        "inputs": normal_values(seeds[0], (BATCH, SEQ, D), 1.0, 6.0, ((0, 16), (1, 2))),
        "doc_lengths": draw_doc_lengths(jax.random.fold_in(seeds[15], 71), 0),
        "qkv_weight": normal_values(seeds[2], (D, 3 * D), (D // 2) ** -0.5, 0.3125, ((0, 2),)),
        "qv_bias": normal_values(seeds[3], (2 * D,), 0.3, 1.796875, ((0, 2),)),
        "out_weight": normal_values(seeds[4], (D, D), (max(D * 16 // SEQ, 1)) ** -0.5, 1.25, ((0, 2),)),
        "out_bias": normal_values(seeds[5], (D,), 0.3, 1.796875, ((0, 2),)),
        "first_gain": jnp.clip(1.0 + 0.1 * jax.random.normal(seeds[6], (D,), jnp.float32), 0.5, 1.5).astype(jnp.bfloat16),
        "first_shift": normal_values(seeds[7], (D,), 0.3, 1.796875, ((0, 2),)),
        "up_weight": normal_values(seeds[8], (D, FF), D ** -0.5, 0.21875, ((0, 2),)),
        "up_bias": normal_values(seeds[9], (FF,), 0.3, 1.796875, ((0, 2),)),
        "down_weight": normal_values(seeds[10], (FF, D), (FF // 2) ** -0.5, 0.15625, ((0, 2),)),
        "down_bias": normal_values(seeds[11], (D,), 0.3, 1.796875, ((0, 2),)),
        "second_gain": jnp.clip(1.0 + 0.1 * jax.random.normal(seeds[12], (D,), jnp.float32), 0.5, 1.5).astype(jnp.bfloat16),
        "second_shift": normal_values(seeds[13], (D,), 0.3, 1.796875, ((0, 2),)),
        "grad_out": normal_values(seeds[14], (BATCH, SEQ, D), 1.0, 6.0, ((0, 16), (1, 2))),
    }


norm_eps = 1e-05
highest = lax.Precision.HIGHEST

@jax.custom_vjp
def low(v):
    return lax.optimization_barrier(v.astype(jnp.bfloat16)).astype(jnp.float32)

@jax.custom_vjp
def low_back(v):
    return v

def low_keep(v):
    return (low(v), None)

def low_pass(kept, grad):
    return (grad,)

def back_keep(v):
    return (v, None)

def back_low(kept, grad):
    return (low(grad),)
low.defvjp(low_keep, low_pass)
low_back.defvjp(back_keep, back_low)

def matmul(left, right):
    return jnp.dot(left, right, precision=highest)

def layer_norm(values, gain, shift):
    center = values - lax.optimization_barrier(jnp.mean(values, axis=-1, keepdims=True))
    spread = lax.optimization_barrier(jnp.mean(center * center, axis=-1, keepdims=True))
    return center * lax.rsqrt(spread + norm_eps) * gain + shift

def doc_ids(lengths):
    ends = jnp.cumsum(lengths)
    spots = jnp.arange(SEQ, dtype=jnp.int32)
    return lax.optimization_barrier(jnp.sum((ends[:, None] <= spots[None, :]).astype(jnp.int32), axis=0))

def forward(tokens, docs, params):
    qkv_weight, qv_bias, out_weight, out_bias, first_gain, first_shift, up_weight, up_bias, down_weight, down_bias, second_gain, second_shift = params
    bias = jnp.concatenate([qv_bias[:D], jnp.zeros((D,), jnp.float32), qv_bias[D:]])
    qkv = low(low_back(matmul(tokens, qkv_weight) + bias))
    query = qkv[:, :D].reshape(SEQ, HEADS, HEAD_DIM)
    keys = qkv[:, D:2 * D].reshape(SEQ, HEADS, HEAD_DIM)
    values = qkv[:, 2 * D:].reshape(SEQ, HEADS, HEAD_DIM)
    scale = 1.0 / jnp.sqrt(jnp.float32(HEAD_DIM))
    scores = low_back(jnp.einsum('qhd,khd->hqk', query, keys, precision=highest) * scale)
    same = (docs[:, None] == docs[None, :])[None]
    masked = jnp.where(same, scores, -1000000000.0)
    top = lax.optimization_barrier(jnp.max(masked, axis=-1, keepdims=True))
    expo = jnp.exp(masked - top)
    probs = expo / lax.optimization_barrier(jnp.sum(expo, axis=-1, keepdims=True))
    mixed = jnp.einsum('hqk,khd->qhd', low(probs), values, precision=highest).reshape(SEQ, D)
    attended = low_back(matmul(low(low_back(mixed)), out_weight) + out_bias)
    first_norm = layer_norm(tokens + attended, first_gain, first_shift)
    hidden = low_back(matmul(low(first_norm), up_weight) + up_bias)
    active = low(jax.nn.gelu(hidden, approximate=False))
    branch = low_back(matmul(active, down_weight) + down_bias)
    return layer_norm(first_norm + branch, second_gain, second_shift)

def reference(inputs, doc_lengths, qkv_weight, qv_bias, out_weight, out_bias, first_gain, first_shift, up_weight, up_bias, down_weight, down_bias, second_gain, second_shift, grad_out):
    params = tuple((p.astype(jnp.float32) for p in (qkv_weight, qv_bias, out_weight, out_bias, first_gain, first_shift, up_weight, up_bias, down_weight, down_bias, second_gain, second_shift)))

    def step(total, item):
        tokens, lengths, cotangent = item
        docs = doc_ids(lengths)

        def run(token_values, param_values):
            return forward(token_values, docs, param_values)
        result, pull = jax.vjp(run, tokens.astype(jnp.float32), params)
        token_grad, param_grad = pull(cotangent.astype(jnp.float32))
        total = jax.tree.map(jnp.add, total, param_grad)
        return (total, (result.astype(jnp.bfloat16), token_grad))
    zeros = jax.tree.map(jnp.zeros_like, params)
    total, (layer_out, input_grad) = lax.scan(step, zeros, (inputs, doc_lengths, grad_out))
    return (layer_out, input_grad, total[0], total[1], total[2], total[3], total[4], total[5], total[6], total[7], total[8], total[9], total[10], total[11])
```

```python
import math

import jax
import jax.numpy as jnp
from jax import lax
from jax.experimental import pallas as pl
from jax.experimental.pallas import tpu as pltpu
from jax.sharding import PartitionSpec as P

HEADS = 12


norm_eps = 1e-05


def norm_forward(values, gain, shift):
    center = values - jnp.mean(values, axis=-1, keepdims=True)
    spread = jnp.mean(center * center, axis=-1, keepdims=True)
    scaler = lax.rsqrt(spread + norm_eps)
    normed = center * scaler
    return (normed * gain + shift, normed, scaler)


def norm_backward(grad, normed, scaler, gain):
    scaled = grad * gain
    inner = scaled - jnp.mean(scaled, axis=-1, keepdims=True)
    inner = inner - normed * jnp.mean(scaled * normed, axis=-1, keepdims=True)
    return inner * scaler


def column_sums(values):
    return jnp.sum(values.astype(jnp.float32), axis=0)


def back_scores(query_seq, keys_seq, values_seq, doc_rows, doc_cols, logsum_seq, grad_seq, scale):
    scores = (
        jnp.einsum("qhd,khd->hqk", query_seq, keys_seq, preferred_element_type=jnp.float32) * scale
    )
    same = (doc_rows[:, None] == doc_cols[None, :])[None]
    probs = jnp.where(same, jnp.exp(scores - logsum_seq), 0.0)
    grad_probs = jnp.einsum(
        "qhd,khd->hqk", grad_seq, values_seq, preferred_element_type=jnp.float32
    )
    return (probs, grad_probs)


def local(
    inputs,
    doc_lengths,
    qkv_weight,
    qv_bias,
    out_weight,
    out_bias,
    first_gain,
    first_shift,
    up_weight,
    up_bias,
    down_weight,
    down_bias,
    second_gain,
    second_shift,
    grad_out,
):
    seqs, rows, width = inputs.shape
    parts = lax.axis_size("shard")
    full_len = rows * parts
    head_dim = width // HEADS
    scale = 1.0 / math.sqrt(head_dim)
    ends = jnp.cumsum(doc_lengths, axis=1)
    spots = jnp.arange(full_len, dtype=jnp.int32)
    doc_all = jnp.sum((ends[:, :, None] <= spots[None, None, :]).astype(jnp.int32), axis=1)
    doc_own = lax.dynamic_slice_in_dim(doc_all, lax.axis_index("shard") * rows, rows, 1)
    gathered = (
        lax.all_gather(qkv_weight, "shard", axis=0, tiled=True),
        lax.all_gather(qv_bias, "shard", axis=0, tiled=True),
        lax.all_gather(out_weight, "shard", axis=0, tiled=True),
        lax.all_gather(out_bias, "shard", axis=0, tiled=True),
        lax.all_gather(first_gain, "shard", axis=0, tiled=True),
        lax.all_gather(first_shift, "shard", axis=0, tiled=True),
        lax.all_gather(up_weight, "shard", axis=0, tiled=True),
        lax.all_gather(up_bias, "shard", axis=0, tiled=True),
        lax.all_gather(down_weight, "shard", axis=0, tiled=True),
        lax.all_gather(down_bias, "shard", axis=0, tiled=True),
        lax.all_gather(second_gain, "shard", axis=0, tiled=True),
        lax.all_gather(second_shift, "shard", axis=0, tiled=True),
    )
    (
        full_qkv,
        full_qv,
        full_out,
        full_outb,
        full_g1,
        full_s1,
        full_up,
        full_upb,
        full_down,
        full_downb,
        full_g2,
        full_s2,
    ) = gathered
    flat = inputs.reshape(seqs * rows, width)
    bias = jnp.concatenate(
        [
            full_qv[:width].astype(jnp.float32),
            jnp.zeros((width,), jnp.float32),
            full_qv[width:].astype(jnp.float32),
        ]
    )
    qkv = (jnp.dot(flat, full_qkv, preferred_element_type=jnp.float32) + bias).astype(jnp.bfloat16)
    query_flat = qkv[:, :width].reshape(seqs, rows, width)
    query = query_flat.reshape(seqs, rows, HEADS, head_dim)
    keys_own = qkv[:, width : 2 * width].reshape(seqs, rows, width)
    values_own = qkv[:, 2 * width :].reshape(seqs, rows, width)
    keys_all, values_all = (
        lax.all_gather(keys_own, "shard", axis=1, tiled=True),
        lax.all_gather(values_own, "shard", axis=1, tiled=True),
    )
    keys_all = keys_all.reshape(seqs, full_len, HEADS, head_dim)
    values_all = values_all.reshape(seqs, full_len, HEADS, head_dim)

    def attend(item):
        query_seq, keys_seq, values_seq, doc_rows, doc_cols = item
        scores = (
            jnp.einsum("qhd,khd->hqk", query_seq, keys_seq, preferred_element_type=jnp.float32)
            * scale
        )
        same = (doc_rows[:, None] == doc_cols[None, :])[None]
        masked = jnp.where(same, scores, -1000000000.0)
        top = jnp.max(masked, axis=-1, keepdims=True)
        expo = jnp.exp(masked - top)
        total = jnp.sum(expo, axis=-1, keepdims=True)
        probs_low = (expo / total).astype(jnp.bfloat16)
        mixed_seq = jnp.einsum(
            "hqk,khd->qhd", probs_low, values_seq, preferred_element_type=jnp.float32
        )
        return (mixed_seq.astype(jnp.bfloat16), top + jnp.log(total))

    mixed, logsum = lax.map(attend, (query, keys_all, values_all, doc_own, doc_all))
    mixed_flat = mixed.reshape(seqs * rows, width)
    attended = jnp.dot(mixed_flat, full_out, preferred_element_type=jnp.float32) + full_outb.astype(
        jnp.float32
    )
    first_norm, first_normed, first_scaler = norm_forward(
        flat.astype(jnp.float32) + attended,
        full_g1.astype(jnp.float32),
        full_s1.astype(jnp.float32),
    )
    first_low = first_norm.astype(jnp.bfloat16)
    hidden = jnp.dot(first_low, full_up, preferred_element_type=jnp.float32) + full_upb.astype(
        jnp.float32
    )
    active = jax.nn.gelu(hidden, approximate=False).astype(jnp.bfloat16)
    branch = jnp.dot(active, full_down, preferred_element_type=jnp.float32) + full_downb.astype(
        jnp.float32
    )
    second_out, second_normed, second_scaler = norm_forward(
        first_norm + branch, full_g2.astype(jnp.float32), full_s2.astype(jnp.float32)
    )
    layer_out = second_out.astype(jnp.bfloat16).reshape(seqs, rows, width)
    back_qkv, back_out, back_g1, back_up, back_down, back_g2 = (
        full_qkv,
        full_out,
        full_g1,
        full_up,
        full_down,
        full_g2,
    )
    cotangent = grad_out.reshape(seqs * rows, width).astype(jnp.float32)
    second_gain_grad = jnp.sum(cotangent * second_normed, axis=0)
    second_shift_grad = jnp.sum(cotangent, axis=0)
    grad_second = norm_backward(
        cotangent, second_normed, second_scaler, back_g2.astype(jnp.float32)
    )
    grad_branch = grad_second.astype(jnp.bfloat16)
    down_weight_grad = jnp.einsum(
        "tf,td->fd", active, grad_branch, preferred_element_type=jnp.float32
    )
    down_bias_grad = column_sums(grad_branch)
    grad_active = jnp.einsum(
        "td,fd->tf", grad_branch, back_down, preferred_element_type=jnp.float32
    )
    normal_cdf = 0.5 * (1.0 + lax.erf(hidden * 0.7071067811865476))
    normal_pdf = jnp.exp(-0.5 * hidden * hidden) * 0.3989422804014327
    grad_hidden = (grad_active * (normal_cdf + hidden * normal_pdf)).astype(jnp.bfloat16)
    up_weight_grad = jnp.einsum(
        "td,tf->df", first_low, grad_hidden, preferred_element_type=jnp.float32
    )
    up_bias_grad = column_sums(grad_hidden)
    grad_first_norm = grad_second + jnp.einsum(
        "tf,df->td", grad_hidden, back_up, preferred_element_type=jnp.float32
    )
    first_gain_grad = jnp.sum(grad_first_norm * first_normed, axis=0)
    first_shift_grad = jnp.sum(grad_first_norm, axis=0)
    grad_first = norm_backward(
        grad_first_norm, first_normed, first_scaler, back_g1.astype(jnp.float32)
    )
    grad_attended = grad_first.astype(jnp.bfloat16)
    out_weight_grad = jnp.einsum(
        "td,te->de", mixed_flat, grad_attended, preferred_element_type=jnp.float32
    )
    out_bias_grad = column_sums(grad_attended)
    grad_mixed = jnp.einsum(
        "te,de->td", grad_attended, back_out, preferred_element_type=jnp.float32
    )
    grad_mixed_flat = grad_mixed.astype(jnp.bfloat16).reshape(seqs, rows, width)
    grad_mixed = grad_mixed_flat.reshape(seqs, rows, HEADS, head_dim)

    def attend_back(item):
        query_seq, keys_seq, values_seq, doc_rows, doc_cols, logsum_seq, grad_seq = item
        probs, grad_probs = back_scores(
            query_seq, keys_seq, values_seq, doc_rows, doc_cols, logsum_seq, grad_seq, scale
        )
        probs_low = probs.astype(jnp.bfloat16)
        inner = jnp.sum(probs * grad_probs, axis=-1, keepdims=True)
        grad_scores = (probs * (grad_probs - inner)).astype(jnp.bfloat16)
        grad_query = (
            jnp.einsum("hqk,khd->qhd", grad_scores, keys_seq, preferred_element_type=jnp.float32)
            * scale
        )
        grad_keys = (
            jnp.einsum("hqk,qhd->khd", grad_scores, query_seq, preferred_element_type=jnp.float32)
            * scale
        )
        grad_values = jnp.einsum(
            "hqk,qhd->khd", probs_low, grad_seq, preferred_element_type=jnp.float32
        )
        return (grad_query, grad_keys, grad_values)

    grad_query, grad_keys, grad_values = lax.map(
        attend_back, (query, keys_all, values_all, doc_own, doc_all, logsum, grad_mixed)
    )
    grad_keys = grad_keys.reshape(seqs, full_len, width)
    grad_values = grad_values.reshape(seqs, full_len, width)
    grad_keys, grad_values = (
        lax.psum_scatter(grad_keys, "shard", scatter_dimension=1, tiled=True),
        lax.psum_scatter(grad_values, "shard", scatter_dimension=1, tiled=True),
    )
    grad_qkv = jnp.concatenate(
        [
            grad_query.reshape(seqs * rows, width),
            grad_keys.reshape(seqs * rows, width),
            grad_values.reshape(seqs * rows, width),
        ],
        axis=1,
    ).astype(jnp.bfloat16)
    qkv_weight_grad = jnp.einsum("td,te->de", flat, grad_qkv, preferred_element_type=jnp.float32)
    qkv_sums = column_sums(grad_qkv)
    qv_bias_grad = jnp.concatenate([qkv_sums[:width], qkv_sums[2 * width :]])
    input_grad = grad_first + jnp.einsum(
        "te,de->td", grad_qkv, back_qkv, preferred_element_type=jnp.float32
    )
    input_grad = input_grad.reshape(seqs, rows, width)
    owned = (
        lax.psum_scatter(qkv_weight_grad, "shard", scatter_dimension=0, tiled=True),
        lax.psum_scatter(qv_bias_grad, "shard", scatter_dimension=0, tiled=True),
        lax.psum_scatter(out_weight_grad, "shard", scatter_dimension=0, tiled=True),
        lax.psum_scatter(out_bias_grad, "shard", scatter_dimension=0, tiled=True),
        lax.psum_scatter(first_gain_grad, "shard", scatter_dimension=0, tiled=True),
        lax.psum_scatter(first_shift_grad, "shard", scatter_dimension=0, tiled=True),
        lax.psum_scatter(up_weight_grad, "shard", scatter_dimension=0, tiled=True),
        lax.psum_scatter(up_bias_grad, "shard", scatter_dimension=0, tiled=True),
        lax.psum_scatter(down_weight_grad, "shard", scatter_dimension=0, tiled=True),
        lax.psum_scatter(down_bias_grad, "shard", scatter_dimension=0, tiled=True),
        lax.psum_scatter(second_gain_grad, "shard", scatter_dimension=0, tiled=True),
        lax.psum_scatter(second_shift_grad, "shard", scatter_dimension=0, tiled=True),
    )
    (
        own_qkv,
        own_qv,
        own_out,
        own_outb,
        own_g1,
        own_s1,
        own_up,
        own_upb,
        own_down,
        own_downb,
        own_g2,
        own_s2,
    ) = owned
    banded = (
        lax.psum_scatter(own_qkv, "rep", scatter_dimension=1, tiled=True),
        lax.psum_scatter(own_out, "rep", scatter_dimension=1, tiled=True),
        lax.psum_scatter(own_up, "rep", scatter_dimension=1, tiled=True),
        lax.psum_scatter(own_down, "rep", scatter_dimension=1, tiled=True),
    )
    matrices = (
        lax.all_gather(banded[0], "rep", axis=1, tiled=True),
        lax.all_gather(banded[1], "rep", axis=1, tiled=True),
        lax.all_gather(banded[2], "rep", axis=1, tiled=True),
        lax.all_gather(banded[3], "rep", axis=1, tiled=True),
    )
    smalls = lax.psum((own_qv, own_outb, own_g1, own_s1, own_upb, own_downb, own_g2, own_s2), "rep")
    return (
        layer_out,
        input_grad,
        matrices[0],
        smalls[0],
        matrices[1],
        smalls[1],
        smalls[2],
        smalls[3],
        matrices[2],
        smalls[4],
        matrices[3],
        smalls[5],
        smalls[6],
        smalls[7],
    )


LOW = jnp.bfloat16
FULL = jnp.float32
MESH = pl.DeviceIdType.MESH
BLOCK = 384
CHUNKS = 12
HOPS = 9
VMEM_GRANT = 60 * 1024 * 1024


def greet(partners):
    barrier = pltpu.get_barrier_semaphore()
    for partner in partners:
        pl.semaphore_signal(barrier, inc=1, device_id=partner, device_id_type=MESH)
    pl.semaphore_wait(barrier, len(partners))


def places():
    rep = lax.axis_index("rep")
    y = lax.axis_index("shard")
    core = lax.rem(rep, 2)
    x = lax.rem(rep // 2, 2)
    z0 = lax.rem(rep // 4, 2)
    z1 = rep // 8
    partners = {
        "core": {"rep": rep + 1 - 2 * core},
        "x": {"rep": rep + 2 - 4 * x},
        "z0": {"rep": rep + 4 - 8 * z0},
        "z1": {"rep": rep + 8 - 16 * z1},
        "y": {"shard": 1 - y},
    }
    return core, x, y, z0, z1, partners


def gather_kernel(
    x_in, g_in, s_in, q_in, o_in, u_in, d_in,
    x_out, g_out, s_out, q_out, o_out, u_out, d_out,
    send, recv, near,
):
    core, x, y, _, _, partners = places()
    rows = x_in.shape[1]
    used = [0]

    def remote(src, dst, way):
        spot = used[0]
        used[0] += 1
        return pltpu.make_async_remote_copy(
            src_ref=src,
            dst_ref=dst,
            send_sem=send.at[spot],
            recv_sem=recv.at[spot],
            device_id=partners[way],
            device_id_type=MESH,
        )

    greet([partners["y"], partners["x"], partners["core"]])

    pieces = []
    for src, dst, parts in ((q_in, q_out, 1), (o_in, o_out, 1), (u_in, u_out, 2), (d_in, d_out, 2)):
        height = src.shape[0]
        size = height // 4 // parts
        for part in range(parts):
            pieces.append((src, dst, height, size, part * size))

    def spot_of(height, size, shift, shard, x_of):
        quarter = 2 * x_of + core
        return pl.ds(shard * height + quarter * (height // 4) + shift, size)

    singles = [
        remote(s_in, s_out.at[y], "y"),
        remote(x_in.at[1 - y], x_out.at[pl.ds(y * rows, rows)], "y"),
    ]
    for copy in singles:
        copy.start()
    over_y = []
    for src, dst, height, size, shift in pieces:
        copy = remote(
            src.at[spot_of(height, size, shift, 0, x)],
            dst.at[spot_of(height, size, shift, y, x)],
            "y",
        )
        copy.start()
        over_y.append(copy)
    last = remote(g_in.at[1 - y], g_out.at[pl.ds(y * rows, rows)], "y")
    last.start()
    singles.append(last)

    locals_ = [
        (s_in, s_out.at[y]),
        (x_in.at[y], x_out.at[pl.ds(y * rows, rows)]),
        (q_in, q_out.at[pl.ds(y * q_in.shape[0], q_in.shape[0])]),
        (o_in, o_out.at[pl.ds(y * o_in.shape[0], o_in.shape[0])]),
        (u_in, u_out.at[pl.ds(y * u_in.shape[0], u_in.shape[0])]),
        (d_in, d_out.at[pl.ds(y * d_in.shape[0], d_in.shape[0])]),
        (g_in.at[y], g_out.at[pl.ds(y * rows, rows)]),
    ]
    locals_ = [pltpu.make_async_copy(a, b, near.at[i]) for i, (a, b) in enumerate(locals_)]
    for copy in locals_:
        copy.start()

    over_x = []
    over_core = []
    for index in range(len(pieces) + 1):
        if index < len(pieces):
            _, dst, height, size, shift = pieces[index]
            over_y[index].wait()
            block = dst.at[spot_of(height, size, shift, 1 - y, x)]
            copy = remote(block, block, "x")
            copy.start()
            over_x.append(copy)
            copy = remote(block, block, "core")
            copy.start()
            over_core.append(copy)
        if index > 0:
            _, dst, height, size, shift = pieces[index - 1]
            over_x[index - 1].wait()
            block = dst.at[spot_of(height, size, shift, 1 - y, 1 - x)]
            copy = remote(block, block, "core")
            copy.start()
            over_core.append(copy)
    for copy in singles + over_core + locals_:
        copy.wait()


def gather_call(x, g, s, q, o, u, d):
    def doubled(a):
        return jax.ShapeDtypeStruct((2 * a.shape[0],) + a.shape[1:], a.dtype)

    tokens = jax.ShapeDtypeStruct((x.shape[0] * x.shape[1], x.shape[2]), x.dtype)
    smalls = jax.ShapeDtypeStruct((2,) + s.shape, s.dtype)
    anywhere = pl.BlockSpec(memory_space=pl.ANY)
    return pl.pallas_call(
        gather_kernel,
        out_shape=(tokens, tokens, smalls, doubled(q), doubled(o), doubled(u), doubled(d)),
        in_specs=[anywhere] * 7,
        out_specs=[anywhere] * 7,
        scratch_shapes=[
            pltpu.SemaphoreType.DMA((27,)),
            pltpu.SemaphoreType.DMA((27,)),
            pltpu.SemaphoreType.DMA((7,)),
        ],
        compiler_params=pltpu.CompilerParams(collective_id=0, has_side_effects=True),
    )(x, g, s, q, o, u, d)


def reduce_kernel(
    low1, gh, act, gb, flat, gqkv, mixed, ga, smalls, ig,
    up_out, down_out, qkv_out, out_out, smalls_out, ig_out,
    parts, got_core, got_y, got_x, got_z0, got_z1, whole, small_now, small_sum, small_got,
    send, recv, small_send, small_recv, ig_send, ig_recv, near,
):
    core, x, y, z0, z1, partners = places()
    rows = ig.shape[0] // 2

    greet([partners[way] for way in ("core", "x", "y", "z0", "z1")])

    ig_copy = pltpu.make_async_remote_copy(
        src_ref=ig.at[pl.ds((1 - y) * rows, rows)],
        dst_ref=ig_out,
        send_sem=ig_send,
        recv_sem=ig_recv,
        device_id=partners["y"],
        device_id_type=MESH,
    )
    ig_copy.start()

    row_x = x * 192
    row_z0 = row_x + z0 * 96
    row_z1 = row_z0 + z1 * 48

    def hop(stage, k):
        if stage == 0:
            pair = (parts.at[k, 1 - core], got_core.at[k], "core")
        elif stage == 1:
            pair = (parts.at[k, core, 1 - y], got_y.at[k], "y")
        elif stage == 2:
            pair = (parts.at[k, core, y, pl.ds((1 - x) * 192, 192)], got_x.at[k], "x")
        elif stage == 3:
            pair = (parts.at[k, core, y, pl.ds(row_x + (1 - z0) * 96, 96)], got_z0.at[k], "z0")
        elif stage == 4:
            pair = (parts.at[k, core, y, pl.ds(row_z0 + (1 - z1) * 48, 48)], got_z1.at[k], "z1")
        elif stage == 5:
            block = whole.at[k, core, pl.ds(row_z1, 48)]
            pair = (block, block, "z1")
        elif stage == 6:
            block = whole.at[k, core, pl.ds(row_z0, 96)]
            pair = (block, block, "z0")
        elif stage == 7:
            block = whole.at[k, core, pl.ds(row_x, 192)]
            pair = (block, block, "x")
        else:
            block = whole.at[k, core]
            pair = (block, block, "core")
        return pltpu.make_async_remote_copy(
            src_ref=pair[0],
            dst_ref=pair[1],
            send_sem=send.at[stage, k],
            recv_sem=recv.at[stage, k],
            device_id=partners[pair[2]],
            device_id_type=MESH,
        )

    def product(k, left, left_spots, right, right_spot):
        for half in range(2):
            lhs = left[:, pl.ds(left_spots[half], BLOCK)]
            for side in range(2):
                spot = right_spot + side * BLOCK
                if not isinstance(spot, int):
                    spot = pl.multiple_of(spot, 128)
                rhs = right[:, pl.ds(spot, BLOCK)]
                parts[k, side, half] = lax.dot_general(
                    lhs, rhs, (((0,), (0,)), ((), ())), preferred_element_type=FULL
                ).astype(LOW)

    def store(k, wait):
        def go(out, row, column):
            for side in range(2):
                copy = pltpu.make_async_copy(
                    whole.at[k, side],
                    out.at[pl.ds(row, BLOCK), pl.ds(pl.multiple_of(column + side * BLOCK, 128), BLOCK)],
                    near.at[k, side],
                )
                if wait:
                    copy.wait()
                else:
                    copy.start()

        @pl.when(k < 4)
        def _():
            go(up_out, 0, k * 768)

        @pl.when((k >= 4) & (k < 8))
        def _():
            go(down_out, (k - 4) * BLOCK, 0)

        @pl.when((k >= 8) & (k < 11))
        def _():
            go(qkv_out, 0, (k - 8) * 768)

        @pl.when(k == 11)
        def _():
            go(out_out, 0, 0)

    def compute(k):
        @pl.when(k < 4)
        def _():
            product(k, low1, (0, BLOCK), gh, k * 768)

        @pl.when((k >= 4) & (k < 8))
        def _():
            spot = pl.multiple_of((k - 4) * BLOCK, 128)
            product(k, act, (spot, pl.multiple_of(spot + 4 * BLOCK, 128)), gb, 0)

        @pl.when((k >= 8) & (k < 11))
        def _():
            product(k, flat, (0, BLOCK), gqkv, (k - 8) * 768)

        @pl.when(k == 11)
        def _():
            product(k, mixed, (0, BLOCK), ga, 0)

    def act_on(stage, k):
        if stage == 0:
            compute(k)
        else:
            hop(stage - 1, k).wait()
        if stage == 1:
            for half in range(2):
                parts[k, core, half] = parts[k, core, half] + got_core[k, half]
        elif stage == 2:
            parts[k, core, y] = parts[k, core, y] + got_y[k]
        elif stage == 3:
            spot = pl.ds(pl.multiple_of(row_x, 16), 192)
            parts[k, core, y, spot] = parts[k, core, y, spot] + got_x[k]
        elif stage == 4:
            spot = pl.ds(pl.multiple_of(row_z0, 16), 96)
            parts[k, core, y, spot] = parts[k, core, y, spot] + got_z0[k]
        elif stage == 5:
            spot = pl.ds(pl.multiple_of(row_z1, 16), 48)
            whole[k, core, spot] = parts[k, core, y, spot] + got_z1[k]
        if stage < HOPS:
            hop(stage, k).start()
        else:
            store(k, False)

    small_now[...] = smalls[...]
    small_ways = ("core", "y", "x", "z0", "z1")

    def small_hop(stage):
        if stage == 0:
            src, dst = small_now, small_got.at[0]
        elif stage == 1:
            src, dst = small_now.at[1 - y], small_got.at[1, 0]
        else:
            src, dst = small_sum.at[stage - 2], small_got.at[stage, 0]
        return pltpu.make_async_remote_copy(
            src_ref=src,
            dst_ref=dst,
            send_sem=small_send.at[stage],
            recv_sem=small_recv.at[stage],
            device_id=partners[small_ways[stage]],
            device_id_type=MESH,
        )

    def small_step(stage):
        if stage > 0:
            small_hop(stage - 1).wait()
        if stage == 1:
            small_now[...] = small_now[...] + small_got[0]
        elif stage == 2:
            small_sum[0] = small_now[y] + small_got[1, 0]
        elif stage in (3, 4):
            small_sum[stage - 2] = small_sum[stage - 3] + small_got[stage - 1, 0]
        elif stage == 5:
            smalls_out[...] = small_sum[2] + small_got[4, 0]
        if stage < 5:
            small_hop(stage).start()

    def turn(t, carry):
        for stage in range(HOPS + 1):
            @pl.when((t >= stage) & (t < stage + CHUNKS))
            def _(stage=stage):
                act_on(stage, t - stage)

        for stage in range(6):
            @pl.when(t == stage)
            def _(stage=stage):
                small_step(stage)

        return carry

    lax.fori_loop(0, CHUNKS + HOPS, turn, 0)

    def finish(k, carry):
        store(k, True)
        return carry

    lax.fori_loop(0, CHUNKS, finish, 0)
    ig_copy.wait()


def reduce_call(low1, gh, act, gb, flat, gqkv, mixed, ga, smalls, ig):
    width = flat.shape[1]
    inside = pl.BlockSpec(memory_space=pltpu.VMEM)
    anywhere = pl.BlockSpec(memory_space=pl.ANY)
    half = (ig.shape[0] // 2, width)
    return pl.pallas_call(
        reduce_kernel,
        out_shape=(
            jax.ShapeDtypeStruct((width // 2, gh.shape[1]), LOW),
            jax.ShapeDtypeStruct((act.shape[1] // 2, width), LOW),
            jax.ShapeDtypeStruct((width // 2, gqkv.shape[1]), LOW),
            jax.ShapeDtypeStruct((width // 2, width), LOW),
            jax.ShapeDtypeStruct(smalls.shape[1:], FULL),
            jax.ShapeDtypeStruct(half, LOW),
        ),
        in_specs=[inside] * 10,
        out_specs=[anywhere] * 4 + [inside, anywhere],
        scratch_shapes=[
            pltpu.VMEM((CHUNKS, 2, 2, BLOCK, BLOCK), LOW),
            pltpu.VMEM((CHUNKS, 2, BLOCK, BLOCK), LOW),
            pltpu.VMEM((CHUNKS, BLOCK, BLOCK), LOW),
            pltpu.VMEM((CHUNKS, 192, BLOCK), LOW),
            pltpu.VMEM((CHUNKS, 96, BLOCK), LOW),
            pltpu.VMEM((CHUNKS, 48, BLOCK), LOW),
            pltpu.VMEM((CHUNKS, 2, BLOCK, BLOCK), LOW),
            pltpu.VMEM(smalls.shape, FULL),
            pltpu.VMEM((3,) + smalls.shape[1:], FULL),
            pltpu.VMEM((5,) + smalls.shape, FULL),
            pltpu.SemaphoreType.DMA((HOPS, CHUNKS)),
            pltpu.SemaphoreType.DMA((HOPS, CHUNKS)),
            pltpu.SemaphoreType.DMA((5,)),
            pltpu.SemaphoreType.DMA((5,)),
            pltpu.SemaphoreType.DMA,
            pltpu.SemaphoreType.DMA,
            pltpu.SemaphoreType.DMA((CHUNKS, 2)),
        ],
        compiler_params=pltpu.CompilerParams(
            collective_id=1, has_side_effects=True, vmem_limit_bytes=VMEM_GRANT
        ),
    )(low1, gh, act, gb, flat, gqkv, mixed, ga, smalls, ig)


def whole_sequence(
    inputs,
    doc_lengths,
    qkv_weight,
    qv_bias,
    out_weight,
    out_bias,
    first_gain,
    first_shift,
    up_weight,
    up_bias,
    down_weight,
    down_bias,
    second_gain,
    second_shift,
    grad_out,
):
    seqs, rows, width = inputs.shape
    full_len = seqs * rows
    y = lax.axis_index("shard")
    head_dim = width // HEADS
    scale = 1.0 / math.sqrt(head_dim)
    vectors = (
        qv_bias, out_bias, first_gain, first_shift, up_bias, down_bias, second_gain, second_shift
    )
    sizes = [v.shape[0] for v in vectors]
    packed = jnp.concatenate(vectors).reshape(12, BLOCK)
    packed = jnp.pad(packed, ((0, 4), (0, 0)))
    flat, cotangent, smalls, full_qkv, full_out, full_up, full_down = gather_call(
        inputs, grad_out, packed, qkv_weight, out_weight, up_weight, down_weight
    )
    smalls = smalls[:, :12].reshape(2, 12 * BLOCK).astype(FULL)
    whole = []
    start = 0
    for size in sizes:
        whole.append(smalls[:, start : start + size].reshape(2 * size))
        start += size
    full_qv, full_outb, full_g1, full_s1, full_upb, full_downb, full_g2, full_s2 = whole
    lengths = lax.dynamic_index_in_dim(doc_lengths, y, 0, keepdims=False)
    ends = jnp.cumsum(lengths)
    spots = jnp.arange(full_len, dtype=jnp.int32)
    docs = jnp.sum((ends[:, None] <= spots[None, :]).astype(jnp.int32), axis=0)
    bias = jnp.concatenate([full_qv[:width], jnp.zeros((width,), FULL), full_qv[width:]])
    qkv = (jnp.dot(flat, full_qkv, preferred_element_type=FULL) + bias).astype(LOW)

    def heads_of(values):
        return values.reshape(full_len, HEADS, head_dim).transpose(1, 0, 2)

    query = heads_of(qkv[:, :width])
    keys = heads_of(qkv[:, width : 2 * width])
    values = heads_of(qkv[:, 2 * width :])
    mixed, logsum = attend_forward(query, keys, values, docs, scale)
    mixed_flat = mixed.transpose(1, 0, 2).reshape(full_len, width)
    attended = jnp.dot(mixed_flat, full_out, preferred_element_type=FULL) + full_outb
    first_norm, first_normed, first_scaler = norm_forward(
        flat.astype(FULL) + attended, full_g1, full_s1
    )
    first_low = first_norm.astype(LOW)
    hidden = jnp.dot(first_low, full_up, preferred_element_type=FULL) + full_upb
    normal_cdf = 0.5 * (1.0 + lax.erf(hidden * 0.7071067811865476))
    active = (hidden * normal_cdf).astype(LOW)
    branch = jnp.dot(active, full_down, preferred_element_type=FULL) + full_downb
    second_out, second_normed, second_scaler = norm_forward(first_norm + branch, full_g2, full_s2)
    layer_own = second_out.astype(LOW).reshape(seqs, rows, width)
    swap = [(0, 1), (1, 0)]
    layer_got = lax.ppermute(
        lax.dynamic_index_in_dim(layer_own, 1 - y, 0, keepdims=False), "shard", swap
    )
    cotangent = cotangent.astype(FULL)
    second_gain_grad = jnp.sum(cotangent * second_normed, axis=0)
    second_shift_grad = jnp.sum(cotangent, axis=0)
    grad_second = norm_backward(cotangent, second_normed, second_scaler, full_g2)
    grad_branch = grad_second.astype(LOW)
    down_bias_grad = column_sums(grad_branch)
    grad_active = jnp.einsum("td,fd->tf", grad_branch, full_down, preferred_element_type=FULL)
    normal_pdf = jnp.exp(-0.5 * hidden * hidden) * 0.3989422804014327
    grad_hidden = (grad_active * (normal_cdf + hidden * normal_pdf)).astype(LOW)
    up_bias_grad = column_sums(grad_hidden)
    grad_first_norm = grad_second + jnp.einsum(
        "tf,df->td", grad_hidden, full_up, preferred_element_type=FULL
    )
    first_gain_grad = jnp.sum(grad_first_norm * first_normed, axis=0)
    first_shift_grad = jnp.sum(grad_first_norm, axis=0)
    grad_first = norm_backward(grad_first_norm, first_normed, first_scaler, full_g1)
    grad_attended = grad_first.astype(LOW)
    out_bias_grad = column_sums(grad_attended)
    grad_mixed = jnp.einsum(
        "te,de->td", grad_attended, full_out, preferred_element_type=FULL
    ).astype(LOW)
    grad_query, grad_keys, grad_values = attend_backward(
        query, keys, values, docs, logsum, heads_of(grad_mixed), scale
    )

    def flat_of(values):
        return values.transpose(1, 0, 2).reshape(full_len, width)

    grad_qkv = jnp.concatenate(
        [flat_of(grad_query), flat_of(grad_keys), flat_of(grad_values)], axis=1
    )
    qkv_sums = column_sums(grad_qkv)
    qv_bias_grad = jnp.concatenate([qkv_sums[:width], qkv_sums[2 * width :]])
    input_grad = grad_first + jnp.einsum(
        "te,de->td", grad_qkv, full_qkv, preferred_element_type=FULL
    )
    small_grads = (
        qv_bias_grad,
        out_bias_grad,
        first_gain_grad,
        first_shift_grad,
        up_bias_grad,
        down_bias_grad,
        second_gain_grad,
        second_shift_grad,
    )
    small_grads = jnp.concatenate([v.reshape(2, -1) for v in small_grads], axis=1)
    small_grads = jnp.pad(small_grads.reshape(2, 6, width), ((0, 0), (0, 2), (0, 0)))
    up_sum, down_sum, qkv_sum, out_sum, small_sum, grad_got = reduce_call(
        first_low,
        grad_hidden,
        active,
        grad_branch,
        flat,
        grad_qkv,
        mixed_flat,
        grad_attended,
        small_grads,
        input_grad.astype(LOW),
    )
    small_sum = small_sum[:6].reshape(6 * width)
    sums = []
    start = 0
    for size in sizes:
        sums.append(small_sum[start : start + size])
        start += size

    def both(own, got):
        own = lax.dynamic_index_in_dim(own, y, 0, keepdims=False)
        first = jnp.where(y == 0, own, got)
        second = jnp.where(y == 0, got, own)
        return jnp.stack([first, second])

    layer_out = both(layer_own, layer_got)
    input_grad = both(input_grad.reshape(seqs, rows, width), grad_got.astype(FULL))
    return (
        layer_out,
        input_grad,
        qkv_sum.astype(FULL),
        sums[0],
        out_sum.astype(FULL),
        sums[1],
        sums[2],
        sums[3],
        up_sum.astype(FULL),
        sums[4],
        down_sum.astype(FULL),
        sums[5],
        sums[6],
        sums[7],
    )


def attend_forward(query, keys, values, docs, scale):
    scores = jnp.einsum("hqd,hkd->hqk", query, keys, preferred_element_type=FULL) * scale
    same = (docs[:, None] == docs[None, :])[None]
    masked = jnp.where(same, scores, -1000000000.0)
    top = jnp.max(masked, axis=-1, keepdims=True)
    expo = jnp.exp(masked - top)
    total = jnp.sum(expo, axis=-1, keepdims=True)
    probs_low = (expo / total).astype(LOW)
    mixed = jnp.einsum("hqk,hkd->hqd", probs_low, values, preferred_element_type=FULL)
    return mixed.astype(LOW), top + jnp.log(total)


def attend_backward(query, keys, values, docs, logsum, grad, scale):
    scores = jnp.einsum("hqd,hkd->hqk", query, keys, preferred_element_type=FULL) * scale
    same = (docs[:, None] == docs[None, :])[None]
    probs = jnp.where(same, jnp.exp(scores - logsum), 0.0)
    grad_probs = jnp.einsum("hqd,hkd->hqk", grad, values, preferred_element_type=FULL)
    probs_low = probs.astype(LOW)
    inner = jnp.sum(probs * grad_probs, axis=-1, keepdims=True)
    grad_scores = (probs * (grad_probs - inner)).astype(LOW)
    grad_query = jnp.einsum("hqk,hkd->hqd", grad_scores, keys, preferred_element_type=FULL) * scale
    grad_keys = jnp.einsum("hqk,hqd->hkd", grad_scores, query, preferred_element_type=FULL) * scale
    grad_values = jnp.einsum("hqk,hqd->hkd", probs_low, grad, preferred_element_type=FULL)
    return grad_query.astype(LOW), grad_keys.astype(LOW), grad_values.astype(LOW)


def solution(mesh):
    shape = (mesh.shape["rep"], mesh.shape["shard"])
    return jax.shard_map(
        whole_sequence if shape == (16, 2) else local,
        mesh=mesh,
        in_specs=(
            P("rep", "shard", None),
            P("rep", None),
            P("shard", None),
            P("shard"),
            P("shard", None),
            P("shard"),
            P("shard"),
            P("shard"),
            P("shard", None),
            P("shard"),
            P("shard", None),
            P("shard"),
            P("shard"),
            P("shard"),
            P("rep", "shard", None),
        ),
        out_specs=(
            P("rep", "shard", None),
            P("rep", "shard", None),
            P("shard", None),
            P("shard"),
            P("shard", None),
            P("shard"),
            P("shard"),
            P("shard"),
            P("shard", None),
            P("shard"),
            P("shard", None),
            P("shard"),
            P("shard"),
            P("shard"),
        ),
        check_vma=False,
    )
```

```python
import math

import jax
import jax.numpy as jnp
from jax import lax
from jax.experimental import pallas as pl
from jax.experimental.pallas import tpu as pltpu
from jax.sharding import PartitionSpec as P

HEADS = 12


norm_eps = 1e-05


def norm_forward(values, gain, shift):
    center = values - jnp.mean(values, axis=-1, keepdims=True)
    spread = jnp.mean(center * center, axis=-1, keepdims=True)
    scaler = lax.rsqrt(spread + norm_eps)
    normed = center * scaler
    return (normed * gain + shift, normed, scaler)


def norm_backward(grad, normed, scaler, gain):
    scaled = grad * gain
    inner = scaled - jnp.mean(scaled, axis=-1, keepdims=True)
    inner = inner - normed * jnp.mean(scaled * normed, axis=-1, keepdims=True)
    return inner * scaler


def column_sums(values):
    return jnp.sum(values.astype(jnp.float32), axis=0)


def back_scores(query_seq, keys_seq, values_seq, doc_rows, doc_cols, logsum_seq, grad_seq, scale):
    scores = (
        jnp.einsum("qhd,khd->hqk", query_seq, keys_seq, preferred_element_type=jnp.float32) * scale
    )
    same = (doc_rows[:, None] == doc_cols[None, :])[None]
    probs = jnp.where(same, jnp.exp(scores - logsum_seq), 0.0)
    grad_probs = jnp.einsum(
        "qhd,khd->hqk", grad_seq, values_seq, preferred_element_type=jnp.float32
    )
    return (probs, grad_probs)


def local(
    inputs,
    doc_lengths,
    qkv_weight,
    qv_bias,
    out_weight,
    out_bias,
    first_gain,
    first_shift,
    up_weight,
    up_bias,
    down_weight,
    down_bias,
    second_gain,
    second_shift,
    grad_out,
):
    seqs, rows, width = inputs.shape
    parts = lax.axis_size("shard")
    full_len = rows * parts
    head_dim = width // HEADS
    scale = 1.0 / math.sqrt(head_dim)
    ends = jnp.cumsum(doc_lengths, axis=1)
    spots = jnp.arange(full_len, dtype=jnp.int32)
    doc_all = jnp.sum((ends[:, :, None] <= spots[None, None, :]).astype(jnp.int32), axis=1)
    doc_own = lax.dynamic_slice_in_dim(doc_all, lax.axis_index("shard") * rows, rows, 1)
    gathered = (
        lax.all_gather(qkv_weight, "shard", axis=0, tiled=True),
        lax.all_gather(qv_bias, "shard", axis=0, tiled=True),
        lax.all_gather(out_weight, "shard", axis=0, tiled=True),
        lax.all_gather(out_bias, "shard", axis=0, tiled=True),
        lax.all_gather(first_gain, "shard", axis=0, tiled=True),
        lax.all_gather(first_shift, "shard", axis=0, tiled=True),
        lax.all_gather(up_weight, "shard", axis=0, tiled=True),
        lax.all_gather(up_bias, "shard", axis=0, tiled=True),
        lax.all_gather(down_weight, "shard", axis=0, tiled=True),
        lax.all_gather(down_bias, "shard", axis=0, tiled=True),
        lax.all_gather(second_gain, "shard", axis=0, tiled=True),
        lax.all_gather(second_shift, "shard", axis=0, tiled=True),
    )
    (
        full_qkv,
        full_qv,
        full_out,
        full_outb,
        full_g1,
        full_s1,
        full_up,
        full_upb,
        full_down,
        full_downb,
        full_g2,
        full_s2,
    ) = gathered
    flat = inputs.reshape(seqs * rows, width)
    bias = jnp.concatenate(
        [
            full_qv[:width].astype(jnp.float32),
            jnp.zeros((width,), jnp.float32),
            full_qv[width:].astype(jnp.float32),
        ]
    )
    qkv = (jnp.dot(flat, full_qkv, preferred_element_type=jnp.float32) + bias).astype(jnp.bfloat16)
    query_flat = qkv[:, :width].reshape(seqs, rows, width)
    query = query_flat.reshape(seqs, rows, HEADS, head_dim)
    keys_own = qkv[:, width : 2 * width].reshape(seqs, rows, width)
    values_own = qkv[:, 2 * width :].reshape(seqs, rows, width)
    keys_all, values_all = (
        lax.all_gather(keys_own, "shard", axis=1, tiled=True),
        lax.all_gather(values_own, "shard", axis=1, tiled=True),
    )
    keys_all = keys_all.reshape(seqs, full_len, HEADS, head_dim)
    values_all = values_all.reshape(seqs, full_len, HEADS, head_dim)

    def attend(item):
        query_seq, keys_seq, values_seq, doc_rows, doc_cols = item
        scores = (
            jnp.einsum("qhd,khd->hqk", query_seq, keys_seq, preferred_element_type=jnp.float32)
            * scale
        )
        same = (doc_rows[:, None] == doc_cols[None, :])[None]
        masked = jnp.where(same, scores, -1000000000.0)
        top = jnp.max(masked, axis=-1, keepdims=True)
        expo = jnp.exp(masked - top)
        total = jnp.sum(expo, axis=-1, keepdims=True)
        probs_low = (expo / total).astype(jnp.bfloat16)
        mixed_seq = jnp.einsum(
            "hqk,khd->qhd", probs_low, values_seq, preferred_element_type=jnp.float32
        )
        return (mixed_seq.astype(jnp.bfloat16), top + jnp.log(total))

    mixed, logsum = lax.map(attend, (query, keys_all, values_all, doc_own, doc_all))
    mixed_flat = mixed.reshape(seqs * rows, width)
    attended = jnp.dot(mixed_flat, full_out, preferred_element_type=jnp.float32) + full_outb.astype(
        jnp.float32
    )
    first_norm, first_normed, first_scaler = norm_forward(
        flat.astype(jnp.float32) + attended,
        full_g1.astype(jnp.float32),
        full_s1.astype(jnp.float32),
    )
    first_low = first_norm.astype(jnp.bfloat16)
    hidden = jnp.dot(first_low, full_up, preferred_element_type=jnp.float32) + full_upb.astype(
        jnp.float32
    )
    active = jax.nn.gelu(hidden, approximate=False).astype(jnp.bfloat16)
    branch = jnp.dot(active, full_down, preferred_element_type=jnp.float32) + full_downb.astype(
        jnp.float32
    )
    second_out, second_normed, second_scaler = norm_forward(
        first_norm + branch, full_g2.astype(jnp.float32), full_s2.astype(jnp.float32)
    )
    layer_out = second_out.astype(jnp.bfloat16).reshape(seqs, rows, width)
    back_qkv, back_out, back_g1, back_up, back_down, back_g2 = (
        full_qkv,
        full_out,
        full_g1,
        full_up,
        full_down,
        full_g2,
    )
    cotangent = grad_out.reshape(seqs * rows, width).astype(jnp.float32)
    second_gain_grad = jnp.sum(cotangent * second_normed, axis=0)
    second_shift_grad = jnp.sum(cotangent, axis=0)
    grad_second = norm_backward(
        cotangent, second_normed, second_scaler, back_g2.astype(jnp.float32)
    )
    grad_branch = grad_second.astype(jnp.bfloat16)
    down_weight_grad = jnp.einsum(
        "tf,td->fd", active, grad_branch, preferred_element_type=jnp.float32
    )
    down_bias_grad = column_sums(grad_branch)
    grad_active = jnp.einsum(
        "td,fd->tf", grad_branch, back_down, preferred_element_type=jnp.float32
    )
    normal_cdf = 0.5 * (1.0 + lax.erf(hidden * 0.7071067811865476))
    normal_pdf = jnp.exp(-0.5 * hidden * hidden) * 0.3989422804014327
    grad_hidden = (grad_active * (normal_cdf + hidden * normal_pdf)).astype(jnp.bfloat16)
    up_weight_grad = jnp.einsum(
        "td,tf->df", first_low, grad_hidden, preferred_element_type=jnp.float32
    )
    up_bias_grad = column_sums(grad_hidden)
    grad_first_norm = grad_second + jnp.einsum(
        "tf,df->td", grad_hidden, back_up, preferred_element_type=jnp.float32
    )
    first_gain_grad = jnp.sum(grad_first_norm * first_normed, axis=0)
    first_shift_grad = jnp.sum(grad_first_norm, axis=0)
    grad_first = norm_backward(
        grad_first_norm, first_normed, first_scaler, back_g1.astype(jnp.float32)
    )
    grad_attended = grad_first.astype(jnp.bfloat16)
    out_weight_grad = jnp.einsum(
        "td,te->de", mixed_flat, grad_attended, preferred_element_type=jnp.float32
    )
    out_bias_grad = column_sums(grad_attended)
    grad_mixed = jnp.einsum(
        "te,de->td", grad_attended, back_out, preferred_element_type=jnp.float32
    )
    grad_mixed_flat = grad_mixed.astype(jnp.bfloat16).reshape(seqs, rows, width)
    grad_mixed = grad_mixed_flat.reshape(seqs, rows, HEADS, head_dim)

    def attend_back(item):
        query_seq, keys_seq, values_seq, doc_rows, doc_cols, logsum_seq, grad_seq = item
        probs, grad_probs = back_scores(
            query_seq, keys_seq, values_seq, doc_rows, doc_cols, logsum_seq, grad_seq, scale
        )
        probs_low = probs.astype(jnp.bfloat16)
        inner = jnp.sum(probs * grad_probs, axis=-1, keepdims=True)
        grad_scores = (probs * (grad_probs - inner)).astype(jnp.bfloat16)
        grad_query = (
            jnp.einsum("hqk,khd->qhd", grad_scores, keys_seq, preferred_element_type=jnp.float32)
            * scale
        )
        grad_keys = (
            jnp.einsum("hqk,qhd->khd", grad_scores, query_seq, preferred_element_type=jnp.float32)
            * scale
        )
        grad_values = jnp.einsum(
            "hqk,qhd->khd", probs_low, grad_seq, preferred_element_type=jnp.float32
        )
        return (grad_query, grad_keys, grad_values)

    grad_query, grad_keys, grad_values = lax.map(
        attend_back, (query, keys_all, values_all, doc_own, doc_all, logsum, grad_mixed)
    )
    grad_keys = grad_keys.reshape(seqs, full_len, width)
    grad_values = grad_values.reshape(seqs, full_len, width)
    grad_keys, grad_values = (
        lax.psum_scatter(grad_keys, "shard", scatter_dimension=1, tiled=True),
        lax.psum_scatter(grad_values, "shard", scatter_dimension=1, tiled=True),
    )
    grad_qkv = jnp.concatenate(
        [
            grad_query.reshape(seqs * rows, width),
            grad_keys.reshape(seqs * rows, width),
            grad_values.reshape(seqs * rows, width),
        ],
        axis=1,
    ).astype(jnp.bfloat16)
    qkv_weight_grad = jnp.einsum("td,te->de", flat, grad_qkv, preferred_element_type=jnp.float32)
    qkv_sums = column_sums(grad_qkv)
    qv_bias_grad = jnp.concatenate([qkv_sums[:width], qkv_sums[2 * width :]])
    input_grad = grad_first + jnp.einsum(
        "te,de->td", grad_qkv, back_qkv, preferred_element_type=jnp.float32
    )
    input_grad = input_grad.reshape(seqs, rows, width)
    owned = (
        lax.psum_scatter(qkv_weight_grad, "shard", scatter_dimension=0, tiled=True),
        lax.psum_scatter(qv_bias_grad, "shard", scatter_dimension=0, tiled=True),
        lax.psum_scatter(out_weight_grad, "shard", scatter_dimension=0, tiled=True),
        lax.psum_scatter(out_bias_grad, "shard", scatter_dimension=0, tiled=True),
        lax.psum_scatter(first_gain_grad, "shard", scatter_dimension=0, tiled=True),
        lax.psum_scatter(first_shift_grad, "shard", scatter_dimension=0, tiled=True),
        lax.psum_scatter(up_weight_grad, "shard", scatter_dimension=0, tiled=True),
        lax.psum_scatter(up_bias_grad, "shard", scatter_dimension=0, tiled=True),
        lax.psum_scatter(down_weight_grad, "shard", scatter_dimension=0, tiled=True),
        lax.psum_scatter(down_bias_grad, "shard", scatter_dimension=0, tiled=True),
        lax.psum_scatter(second_gain_grad, "shard", scatter_dimension=0, tiled=True),
        lax.psum_scatter(second_shift_grad, "shard", scatter_dimension=0, tiled=True),
    )
    (
        own_qkv,
        own_qv,
        own_out,
        own_outb,
        own_g1,
        own_s1,
        own_up,
        own_upb,
        own_down,
        own_downb,
        own_g2,
        own_s2,
    ) = owned
    banded = (
        lax.psum_scatter(own_qkv, "rep", scatter_dimension=1, tiled=True),
        lax.psum_scatter(own_out, "rep", scatter_dimension=1, tiled=True),
        lax.psum_scatter(own_up, "rep", scatter_dimension=1, tiled=True),
        lax.psum_scatter(own_down, "rep", scatter_dimension=1, tiled=True),
    )
    matrices = (
        lax.all_gather(banded[0], "rep", axis=1, tiled=True),
        lax.all_gather(banded[1], "rep", axis=1, tiled=True),
        lax.all_gather(banded[2], "rep", axis=1, tiled=True),
        lax.all_gather(banded[3], "rep", axis=1, tiled=True),
    )
    smalls = lax.psum((own_qv, own_outb, own_g1, own_s1, own_upb, own_downb, own_g2, own_s2), "rep")
    return (
        layer_out,
        input_grad,
        matrices[0],
        smalls[0],
        matrices[1],
        smalls[1],
        smalls[2],
        smalls[3],
        matrices[2],
        smalls[4],
        matrices[3],
        smalls[5],
        smalls[6],
        smalls[7],
    )


LOW = jnp.bfloat16
FULL = jnp.float32
MESH = pl.DeviceIdType.MESH
BLOCK = 384
CHUNKS = 12
HOPS = 9
VMEM_GRANT = 60 * 1024 * 1024


def greet(partners):
    barrier = pltpu.get_barrier_semaphore()
    for partner in partners:
        pl.semaphore_signal(barrier, inc=1, device_id=partner, device_id_type=MESH)
    pl.semaphore_wait(barrier, len(partners))


def places():
    rep = lax.axis_index("rep")
    y = lax.axis_index("shard")
    core = lax.rem(rep, 2)
    x = lax.rem(rep // 2, 2)
    z0 = lax.rem(rep // 4, 2)
    z1 = rep // 8
    partners = {
        "core": {"rep": rep + 1 - 2 * core},
        "x": {"rep": rep + 2 - 4 * x},
        "z0": {"rep": rep + 4 - 8 * z0},
        "z1": {"rep": rep + 8 - 16 * z1},
        "y": {"shard": 1 - y},
    }
    return core, x, y, z0, z1, partners


def gather_kernel(
    x_in, s_in, q_in, o_in, u_in, d_in,
    x_out, s_out, q_out, o_out, u_out, d_out,
    send, recv,
):
    core, x, y, z0, _, partners = places()
    rows = x_in.shape[1]
    width = x_in.shape[2]
    used = [0]

    def remote(src, dst, way):
        spot = used[0]
        used[0] += 1
        return pltpu.make_async_remote_copy(
            src_ref=src,
            dst_ref=dst,
            send_sem=send.at[spot],
            recv_sem=recv.at[spot],
            device_id=partners[way],
            device_id_type=MESH,
        )

    greet([partners[way] for way in ("y", "x", "z0", "core")])

    pieces = []
    for src, dst in ((q_in, q_out), (o_in, o_out), (u_in, u_out), (d_in, d_out)):
        height = src.shape[0]
        for row in range(0, height, BLOCK):
            for column in range(0, src.shape[1], width):
                pieces.append((src, dst, height, row, pl.ds(column, width)))

    singles = [
        remote(s_in, s_out.at[y], "y"),
        remote(x_in.at[1 - y], x_out.at[pl.ds(y * rows, rows)], "y"),
    ]
    for copy in singles:
        copy.start()

    def place(index):
        outer, inner = (x, z0) if index % 2 == 0 else (z0, x)
        return core * 192 + outer * 96, inner * 48

    over_y = []
    for index, (src, dst, height, row, columns) in enumerate(pieces):
        outer, inner = place(index)
        copy = remote(
            src.at[pl.ds(row + outer + inner, 48), columns],
            dst.at[pl.ds(y * height + row + outer + inner, 48), columns],
            "y",
        )
        copy.start()
        over_y.append(copy)

    s_out[y] = s_in[...]
    x_out[pl.ds(pl.multiple_of(y * rows, 16), rows)] = x_in[y]
    for src, dst in ((q_in, q_out), (o_in, o_out), (u_in, u_out), (d_in, d_out)):
        height = src.shape[0]

        def keep(i, carry, src=src, dst=dst, height=height):
            spot = pl.ds(pl.multiple_of(y * height + i * 48, 16), 48)
            dst[spot] = src[pl.ds(pl.multiple_of(i * 48, 16), 48)]
            return carry

        lax.fori_loop(0, height // 48, keep, 0)

    over_first, over_second, over_core = [], [], []
    count = len(pieces)
    for turn in range(count + 2):
        for stage in range(3):
            index = turn - stage
            if index < 0 or index >= count:
                continue
            _, dst, height, row, columns = pieces[index]
            outer, inner = place(index)
            base = (1 - y) * height + row
            if stage == 0:
                over_y[index].wait()
                block = dst.at[pl.ds(base + outer + inner, 48), columns]
                way, made = ("z0" if index % 2 == 0 else "x"), over_first
            elif stage == 1:
                over_first[index].wait()
                block = dst.at[pl.ds(base + outer, 96), columns]
                way, made = ("x" if index % 2 == 0 else "z0"), over_second
            else:
                over_second[index].wait()
                block = dst.at[pl.ds(base + core * 192, 192), columns]
                way, made = "core", over_core
            copy = remote(block, block, way)
            copy.start()
            made.append(copy)
    for copy in singles + over_core:
        copy.wait()


def gather_call(x, s, q, o, u, d):
    def doubled(a):
        return jax.ShapeDtypeStruct((2 * a.shape[0],) + a.shape[1:], a.dtype)

    tokens = jax.ShapeDtypeStruct((x.shape[0] * x.shape[1], x.shape[2]), x.dtype)
    smalls = jax.ShapeDtypeStruct((2,) + s.shape, s.dtype)
    inside = pl.BlockSpec(memory_space=pltpu.VMEM)
    return pl.pallas_call(
        gather_kernel,
        out_shape=(tokens, smalls, doubled(q), doubled(o), doubled(u), doubled(d)),
        in_specs=[inside] * 6,
        out_specs=[inside] * 6,
        scratch_shapes=[
            pltpu.SemaphoreType.DMA((50,)),
            pltpu.SemaphoreType.DMA((50,)),
        ],
        compiler_params=pltpu.CompilerParams(
            collective_id=0, has_side_effects=True, vmem_limit_bytes=48 * 1024 * 1024
        ),
    )(x, s, q, o, u, d)


def reduce_kernel(
    low1, gh, act, gb, flat, gqkv, mixed, ga, smalls, ig,
    up_out, down_out, qkv_out, out_out, smalls_out, ig_out,
    parts, got_core, got_y, got_x, got_z0, got_z1, whole, small_now, small_sum, small_got,
    send, recv, small_send, small_recv, ig_send, ig_recv, near,
):
    core, x, y, z0, z1, partners = places()
    rows = ig.shape[0] // 2

    greet([partners[way] for way in ("core", "x", "y", "z0", "z1")])

    ig_copy = pltpu.make_async_remote_copy(
        src_ref=ig.at[pl.ds((1 - y) * rows, rows)],
        dst_ref=ig_out,
        send_sem=ig_send,
        recv_sem=ig_recv,
        device_id=partners["y"],
        device_id_type=MESH,
    )
    ig_copy.start()

    row_x = x * 192
    row_z0 = row_x + z0 * 96
    row_z1 = row_z0 + z1 * 48

    def hop(stage, k):
        if stage == 0:
            pair = (parts.at[k, 1 - core], got_core.at[k], "core")
        elif stage == 1:
            pair = (parts.at[k, core, 1 - y], got_y.at[k], "y")
        elif stage == 2:
            pair = (parts.at[k, core, y, pl.ds((1 - x) * 192, 192)], got_x.at[k], "x")
        elif stage == 3:
            pair = (parts.at[k, core, y, pl.ds(row_x + (1 - z0) * 96, 96)], got_z0.at[k], "z0")
        elif stage == 4:
            pair = (parts.at[k, core, y, pl.ds(row_z0 + (1 - z1) * 48, 48)], got_z1.at[k], "z1")
        elif stage == 5:
            block = whole.at[k, core, pl.ds(row_z1, 48)]
            pair = (block, block, "z1")
        elif stage == 6:
            block = whole.at[k, core, pl.ds(row_z0, 96)]
            pair = (block, block, "z0")
        elif stage == 7:
            block = whole.at[k, core, pl.ds(row_x, 192)]
            pair = (block, block, "x")
        else:
            block = whole.at[k, core]
            pair = (block, block, "core")
        return pltpu.make_async_remote_copy(
            src_ref=pair[0],
            dst_ref=pair[1],
            send_sem=send.at[stage, k],
            recv_sem=recv.at[stage, k],
            device_id=partners[pair[2]],
            device_id_type=MESH,
        )

    def product(k, left, left_spots, right, right_spot):
        for half in range(2):
            lhs = left[:, pl.ds(left_spots[half], BLOCK)]
            for side in range(2):
                spot = right_spot + side * BLOCK
                if not isinstance(spot, int):
                    spot = pl.multiple_of(spot, 128)
                rhs = right[:, pl.ds(spot, BLOCK)]
                parts[k, side, half] = lax.dot_general(
                    lhs, rhs, (((0,), (0,)), ((), ())), preferred_element_type=FULL
                ).astype(LOW)

    def store(k, wait):
        def go(out, row, column):
            for side in range(2):
                copy = pltpu.make_async_copy(
                    whole.at[k, side],
                    out.at[pl.ds(row, BLOCK), pl.ds(pl.multiple_of(column + side * BLOCK, 128), BLOCK)],
                    near.at[k, side],
                )
                if wait:
                    copy.wait()
                else:
                    copy.start()

        @pl.when(k < 4)
        def _():
            go(up_out, 0, k * 768)

        @pl.when((k >= 4) & (k < 8))
        def _():
            go(down_out, (k - 4) * BLOCK, 0)

        @pl.when((k >= 8) & (k < 11))
        def _():
            go(qkv_out, 0, (k - 8) * 768)

        @pl.when(k == 11)
        def _():
            go(out_out, 0, 0)

    def compute(k):
        @pl.when(k < 4)
        def _():
            product(k, low1, (0, BLOCK), gh, k * 768)

        @pl.when((k >= 4) & (k < 8))
        def _():
            spot = pl.multiple_of((k - 4) * BLOCK, 128)
            product(k, act, (spot, pl.multiple_of(spot + 4 * BLOCK, 128)), gb, 0)

        @pl.when((k >= 8) & (k < 11))
        def _():
            product(k, flat, (0, BLOCK), gqkv, (k - 8) * 768)

        @pl.when(k == 11)
        def _():
            product(k, mixed, (0, BLOCK), ga, 0)

    def act_on(stage, k):
        if stage == 0:
            compute(k)
        else:
            hop(stage - 1, k).wait()
        if stage == 1:
            for half in range(2):
                parts[k, core, half] = parts[k, core, half] + got_core[k, half]
        elif stage == 2:
            parts[k, core, y] = parts[k, core, y] + got_y[k]
        elif stage == 3:
            spot = pl.ds(pl.multiple_of(row_x, 16), 192)
            parts[k, core, y, spot] = parts[k, core, y, spot] + got_x[k]
        elif stage == 4:
            spot = pl.ds(pl.multiple_of(row_z0, 16), 96)
            parts[k, core, y, spot] = parts[k, core, y, spot] + got_z0[k]
        elif stage == 5:
            spot = pl.ds(pl.multiple_of(row_z1, 16), 48)
            whole[k, core, spot] = parts[k, core, y, spot] + got_z1[k]
        if stage < HOPS:
            hop(stage, k).start()
        else:
            store(k, False)

    small_now[...] = smalls[...]
    small_ways = ("core", "y", "x", "z0", "z1")

    def small_hop(stage):
        if stage == 0:
            src, dst = small_now, small_got.at[0]
        elif stage == 1:
            src, dst = small_now.at[1 - y], small_got.at[1, 0]
        else:
            src, dst = small_sum.at[stage - 2], small_got.at[stage, 0]
        return pltpu.make_async_remote_copy(
            src_ref=src,
            dst_ref=dst,
            send_sem=small_send.at[stage],
            recv_sem=small_recv.at[stage],
            device_id=partners[small_ways[stage]],
            device_id_type=MESH,
        )

    def small_step(stage):
        if stage > 0:
            small_hop(stage - 1).wait()
        if stage == 1:
            small_now[...] = small_now[...] + small_got[0]
        elif stage == 2:
            small_sum[0] = small_now[y] + small_got[1, 0]
        elif stage in (3, 4):
            small_sum[stage - 2] = small_sum[stage - 3] + small_got[stage - 1, 0]
        elif stage == 5:
            smalls_out[...] = small_sum[2] + small_got[4, 0]
        if stage < 5:
            small_hop(stage).start()

    def turn(t, carry):
        for stage in range(HOPS + 1):
            @pl.when((t >= stage) & (t < stage + CHUNKS))
            def _(stage=stage):
                act_on(stage, t - stage)

        for stage in range(6):
            @pl.when(t == stage)
            def _(stage=stage):
                small_step(stage)

        return carry

    lax.fori_loop(0, CHUNKS + HOPS, turn, 0)

    def finish(k, carry):
        store(k, True)
        return carry

    lax.fori_loop(0, CHUNKS, finish, 0)
    ig_copy.wait()


def reduce_call(low1, gh, act, gb, flat, gqkv, mixed, ga, smalls, ig):
    width = flat.shape[1]
    inside = pl.BlockSpec(memory_space=pltpu.VMEM)
    anywhere = pl.BlockSpec(memory_space=pl.ANY)
    half = (ig.shape[0] // 2, width)
    return pl.pallas_call(
        reduce_kernel,
        out_shape=(
            jax.ShapeDtypeStruct((width // 2, gh.shape[1]), LOW),
            jax.ShapeDtypeStruct((act.shape[1] // 2, width), LOW),
            jax.ShapeDtypeStruct((width // 2, gqkv.shape[1]), LOW),
            jax.ShapeDtypeStruct((width // 2, width), LOW),
            jax.ShapeDtypeStruct(smalls.shape[1:], FULL),
            jax.ShapeDtypeStruct(half, LOW),
        ),
        in_specs=[inside] * 10,
        out_specs=[anywhere] * 4 + [inside, anywhere],
        scratch_shapes=[
            pltpu.VMEM((CHUNKS, 2, 2, BLOCK, BLOCK), LOW),
            pltpu.VMEM((CHUNKS, 2, BLOCK, BLOCK), LOW),
            pltpu.VMEM((CHUNKS, BLOCK, BLOCK), LOW),
            pltpu.VMEM((CHUNKS, 192, BLOCK), LOW),
            pltpu.VMEM((CHUNKS, 96, BLOCK), LOW),
            pltpu.VMEM((CHUNKS, 48, BLOCK), LOW),
            pltpu.VMEM((CHUNKS, 2, BLOCK, BLOCK), LOW),
            pltpu.VMEM(smalls.shape, FULL),
            pltpu.VMEM((3,) + smalls.shape[1:], FULL),
            pltpu.VMEM((5,) + smalls.shape, FULL),
            pltpu.SemaphoreType.DMA((HOPS, CHUNKS)),
            pltpu.SemaphoreType.DMA((HOPS, CHUNKS)),
            pltpu.SemaphoreType.DMA((5,)),
            pltpu.SemaphoreType.DMA((5,)),
            pltpu.SemaphoreType.DMA,
            pltpu.SemaphoreType.DMA,
            pltpu.SemaphoreType.DMA((CHUNKS, 2)),
        ],
        compiler_params=pltpu.CompilerParams(
            collective_id=1, has_side_effects=True, vmem_limit_bytes=VMEM_GRANT
        ),
    )(low1, gh, act, gb, flat, gqkv, mixed, ga, smalls, ig)


def whole_sequence(
    inputs,
    doc_lengths,
    qkv_weight,
    qv_bias,
    out_weight,
    out_bias,
    first_gain,
    first_shift,
    up_weight,
    up_bias,
    down_weight,
    down_bias,
    second_gain,
    second_shift,
    grad_out,
):
    seqs, rows, width = inputs.shape
    full_len = seqs * rows
    y = lax.axis_index("shard")
    head_dim = width // HEADS
    scale = 1.0 / math.sqrt(head_dim)
    vectors = (
        qv_bias, out_bias, first_gain, first_shift, up_bias, down_bias, second_gain, second_shift
    )
    sizes = [v.shape[0] for v in vectors]
    packed = jnp.concatenate(vectors).reshape(12, BLOCK)
    packed = jnp.pad(packed, ((0, 4), (0, 0)))
    flat, smalls, full_qkv, full_out, full_up, full_down = gather_call(
        inputs, packed, qkv_weight, out_weight, up_weight, down_weight
    )
    swap = [(0, 1), (1, 0)]
    grad_other = lax.dynamic_index_in_dim(grad_out, 1 - y, 0, keepdims=False)
    grad_other, flat = lax.optimization_barrier((grad_other, flat))
    grad_other = lax.ppermute(grad_other, "shard", swap)
    grad_own = lax.dynamic_index_in_dim(grad_out, y, 0, keepdims=False)
    cotangent = jnp.concatenate(
        [jnp.where(y == 0, grad_own, grad_other), jnp.where(y == 0, grad_other, grad_own)]
    )
    smalls = smalls[:, :12].reshape(2, 12 * BLOCK).astype(FULL)
    whole = []
    start = 0
    for size in sizes:
        whole.append(smalls[:, start : start + size].reshape(2 * size))
        start += size
    full_qv, full_outb, full_g1, full_s1, full_upb, full_downb, full_g2, full_s2 = whole
    lengths = lax.dynamic_index_in_dim(doc_lengths, y, 0, keepdims=False)
    ends = jnp.cumsum(lengths)
    spots = jnp.arange(full_len, dtype=jnp.int32)
    docs = jnp.sum((ends[:, None] <= spots[None, :]).astype(jnp.int32), axis=0)
    bias = jnp.concatenate([full_qv[:width], jnp.zeros((width,), FULL), full_qv[width:]])
    qkv = (jnp.dot(flat, full_qkv, preferred_element_type=FULL) + bias).astype(LOW)

    def heads_of(values):
        return values.reshape(full_len, HEADS, head_dim).transpose(1, 0, 2)

    query = heads_of(qkv[:, :width])
    keys = heads_of(qkv[:, width : 2 * width])
    values = heads_of(qkv[:, 2 * width :])
    mixed, logsum = attend_forward(query, keys, values, docs, scale)
    mixed_flat = mixed.transpose(1, 0, 2).reshape(full_len, width)
    attended = jnp.dot(mixed_flat, full_out, preferred_element_type=FULL) + full_outb
    first_norm, first_normed, first_scaler = norm_forward(
        flat.astype(FULL) + attended, full_g1, full_s1
    )
    first_low = first_norm.astype(LOW)
    hidden = jnp.dot(first_low, full_up, preferred_element_type=FULL) + full_upb
    normal_cdf = 0.5 * (1.0 + lax.erf(hidden * 0.7071067811865476))
    active = (hidden * normal_cdf).astype(LOW)
    branch = jnp.dot(active, full_down, preferred_element_type=FULL) + full_downb
    second_out, second_normed, second_scaler = norm_forward(first_norm + branch, full_g2, full_s2)
    layer_own = second_out.astype(LOW).reshape(seqs, rows, width)
    layer_got = lax.ppermute(
        lax.dynamic_index_in_dim(layer_own, 1 - y, 0, keepdims=False), "shard", swap
    )
    cotangent = cotangent.astype(FULL)
    second_gain_grad = jnp.sum(cotangent * second_normed, axis=0)
    second_shift_grad = jnp.sum(cotangent, axis=0)
    grad_second = norm_backward(cotangent, second_normed, second_scaler, full_g2)
    grad_branch = grad_second.astype(LOW)
    down_bias_grad = column_sums(grad_branch)
    grad_active = jnp.einsum("td,fd->tf", grad_branch, full_down, preferred_element_type=FULL)
    normal_pdf = jnp.exp(-0.5 * hidden * hidden) * 0.3989422804014327
    grad_hidden = (grad_active * (normal_cdf + hidden * normal_pdf)).astype(LOW)
    up_bias_grad = column_sums(grad_hidden)
    grad_first_norm = grad_second + jnp.einsum(
        "tf,df->td", grad_hidden, full_up, preferred_element_type=FULL
    )
    first_gain_grad = jnp.sum(grad_first_norm * first_normed, axis=0)
    first_shift_grad = jnp.sum(grad_first_norm, axis=0)
    grad_first = norm_backward(grad_first_norm, first_normed, first_scaler, full_g1)
    grad_attended = grad_first.astype(LOW)
    out_bias_grad = column_sums(grad_attended)
    grad_mixed = jnp.einsum(
        "te,de->td", grad_attended, full_out, preferred_element_type=FULL
    ).astype(LOW)
    grad_query, grad_keys, grad_values = attend_backward(
        query, keys, values, docs, logsum, heads_of(grad_mixed), scale
    )

    def flat_of(values):
        return values.transpose(1, 0, 2).reshape(full_len, width)

    grad_qkv = jnp.concatenate(
        [flat_of(grad_query), flat_of(grad_keys), flat_of(grad_values)], axis=1
    )
    qkv_sums = column_sums(grad_qkv)
    qv_bias_grad = jnp.concatenate([qkv_sums[:width], qkv_sums[2 * width :]])
    input_grad = grad_first + jnp.einsum(
        "te,de->td", grad_qkv, full_qkv, preferred_element_type=FULL
    )
    small_grads = (
        qv_bias_grad,
        out_bias_grad,
        first_gain_grad,
        first_shift_grad,
        up_bias_grad,
        down_bias_grad,
        second_gain_grad,
        second_shift_grad,
    )
    small_grads = jnp.concatenate([v.reshape(2, -1) for v in small_grads], axis=1)
    small_grads = jnp.pad(small_grads.reshape(2, 6, width), ((0, 0), (0, 2), (0, 0)))
    up_sum, down_sum, qkv_sum, out_sum, small_sum, grad_got = reduce_call(
        first_low,
        grad_hidden,
        active,
        grad_branch,
        flat,
        grad_qkv,
        mixed_flat,
        grad_attended,
        small_grads,
        input_grad.astype(LOW),
    )
    small_sum = small_sum[:6].reshape(6 * width)
    sums = []
    start = 0
    for size in sizes:
        sums.append(small_sum[start : start + size])
        start += size

    def both(own, got):
        own = lax.dynamic_index_in_dim(own, y, 0, keepdims=False)
        first = jnp.where(y == 0, own, got)
        second = jnp.where(y == 0, got, own)
        return jnp.stack([first, second])

    layer_out = both(layer_own, layer_got)
    input_grad = both(input_grad.reshape(seqs, rows, width), grad_got.astype(FULL))
    return (
        layer_out,
        input_grad,
        qkv_sum.astype(FULL),
        sums[0],
        out_sum.astype(FULL),
        sums[1],
        sums[2],
        sums[3],
        up_sum.astype(FULL),
        sums[4],
        down_sum.astype(FULL),
        sums[5],
        sums[6],
        sums[7],
    )


def attend_forward(query, keys, values, docs, scale):
    scores = jnp.einsum("hqd,hkd->hqk", query, keys, preferred_element_type=FULL) * scale
    same = (docs[:, None] == docs[None, :])[None]
    masked = jnp.where(same, scores, -1000000000.0)
    top = jnp.max(masked, axis=-1, keepdims=True)
    expo = jnp.exp(masked - top)
    total = jnp.sum(expo, axis=-1, keepdims=True)
    probs_low = (expo / total).astype(LOW)
    mixed = jnp.einsum("hqk,hkd->hqd", probs_low, values, preferred_element_type=FULL)
    return mixed.astype(LOW), top + jnp.log(total)


def attend_backward(query, keys, values, docs, logsum, grad, scale):
    scores = jnp.einsum("hqd,hkd->hqk", query, keys, preferred_element_type=FULL) * scale
    same = (docs[:, None] == docs[None, :])[None]
    probs = jnp.where(same, jnp.exp(scores - logsum), 0.0)
    grad_probs = jnp.einsum("hqd,hkd->hqk", grad, values, preferred_element_type=FULL)
    probs_low = probs.astype(LOW)
    inner = jnp.sum(probs * grad_probs, axis=-1, keepdims=True)
    grad_scores = (probs * (grad_probs - inner)).astype(LOW)
    grad_query = jnp.einsum("hqk,hkd->hqd", grad_scores, keys, preferred_element_type=FULL) * scale
    grad_keys = jnp.einsum("hqk,hqd->hkd", grad_scores, query, preferred_element_type=FULL) * scale
    grad_values = jnp.einsum("hqk,hqd->hkd", probs_low, grad, preferred_element_type=FULL)
    return grad_query.astype(LOW), grad_keys.astype(LOW), grad_values.astype(LOW)


def solution(mesh):
    shape = (mesh.shape["rep"], mesh.shape["shard"])
    return jax.shard_map(
        whole_sequence if shape == (16, 2) else local,
        mesh=mesh,
        in_specs=(
            P("rep", "shard", None),
            P("rep", None),
            P("shard", None),
            P("shard"),
            P("shard", None),
            P("shard"),
            P("shard"),
            P("shard"),
            P("shard", None),
            P("shard"),
            P("shard", None),
            P("shard"),
            P("shard"),
            P("shard"),
            P("rep", "shard", None),
        ),
        out_specs=(
            P("rep", "shard", None),
            P("rep", "shard", None),
            P("shard", None),
            P("shard"),
            P("shard", None),
            P("shard"),
            P("shard"),
            P("shard"),
            P("shard", None),
            P("shard"),
            P("shard", None),
            P("shard"),
            P("shard"),
            P("shard"),
        ),
        check_vma=False,
    )
```

```python
import functools
import math

import jax
import jax.numpy as jnp
from jax import lax
from jax.experimental import pallas as pl
from jax.experimental.pallas import tpu as pltpu
from jax.sharding import PartitionSpec as P

HEADS = 12


norm_eps = 1e-05


def norm_forward(values, gain, shift):
    center = values - jnp.mean(values, axis=-1, keepdims=True)
    spread = jnp.mean(center * center, axis=-1, keepdims=True)
    scaler = lax.rsqrt(spread + norm_eps)
    normed = center * scaler
    return (normed * gain + shift, normed, scaler)


def norm_backward(grad, normed, scaler, gain):
    scaled = grad * gain
    inner = scaled - jnp.mean(scaled, axis=-1, keepdims=True)
    inner = inner - normed * jnp.mean(scaled * normed, axis=-1, keepdims=True)
    return inner * scaler


def column_sums(values):
    return jnp.sum(values.astype(jnp.float32), axis=0)


def back_scores(query_seq, keys_seq, values_seq, doc_rows, doc_cols, logsum_seq, grad_seq, scale):
    scores = (
        jnp.einsum("qhd,khd->hqk", query_seq, keys_seq, preferred_element_type=jnp.float32) * scale
    )
    same = (doc_rows[:, None] == doc_cols[None, :])[None]
    probs = jnp.where(same, jnp.exp(scores - logsum_seq), 0.0)
    grad_probs = jnp.einsum(
        "qhd,khd->hqk", grad_seq, values_seq, preferred_element_type=jnp.float32
    )
    return (probs, grad_probs)


def local(
    inputs,
    doc_lengths,
    qkv_weight,
    qv_bias,
    out_weight,
    out_bias,
    first_gain,
    first_shift,
    up_weight,
    up_bias,
    down_weight,
    down_bias,
    second_gain,
    second_shift,
    grad_out,
):
    seqs, rows, width = inputs.shape
    parts = lax.axis_size("shard")
    full_len = rows * parts
    head_dim = width // HEADS
    scale = 1.0 / math.sqrt(head_dim)
    ends = jnp.cumsum(doc_lengths, axis=1)
    spots = jnp.arange(full_len, dtype=jnp.int32)
    doc_all = jnp.sum((ends[:, :, None] <= spots[None, None, :]).astype(jnp.int32), axis=1)
    doc_own = lax.dynamic_slice_in_dim(doc_all, lax.axis_index("shard") * rows, rows, 1)
    gathered = (
        lax.all_gather(qkv_weight, "shard", axis=0, tiled=True),
        lax.all_gather(qv_bias, "shard", axis=0, tiled=True),
        lax.all_gather(out_weight, "shard", axis=0, tiled=True),
        lax.all_gather(out_bias, "shard", axis=0, tiled=True),
        lax.all_gather(first_gain, "shard", axis=0, tiled=True),
        lax.all_gather(first_shift, "shard", axis=0, tiled=True),
        lax.all_gather(up_weight, "shard", axis=0, tiled=True),
        lax.all_gather(up_bias, "shard", axis=0, tiled=True),
        lax.all_gather(down_weight, "shard", axis=0, tiled=True),
        lax.all_gather(down_bias, "shard", axis=0, tiled=True),
        lax.all_gather(second_gain, "shard", axis=0, tiled=True),
        lax.all_gather(second_shift, "shard", axis=0, tiled=True),
    )
    (
        full_qkv,
        full_qv,
        full_out,
        full_outb,
        full_g1,
        full_s1,
        full_up,
        full_upb,
        full_down,
        full_downb,
        full_g2,
        full_s2,
    ) = gathered
    flat = inputs.reshape(seqs * rows, width)
    bias = jnp.concatenate(
        [
            full_qv[:width].astype(jnp.float32),
            jnp.zeros((width,), jnp.float32),
            full_qv[width:].astype(jnp.float32),
        ]
    )
    qkv = (jnp.dot(flat, full_qkv, preferred_element_type=jnp.float32) + bias).astype(jnp.bfloat16)
    query_flat = qkv[:, :width].reshape(seqs, rows, width)
    query = query_flat.reshape(seqs, rows, HEADS, head_dim)
    keys_own = qkv[:, width : 2 * width].reshape(seqs, rows, width)
    values_own = qkv[:, 2 * width :].reshape(seqs, rows, width)
    keys_all, values_all = (
        lax.all_gather(keys_own, "shard", axis=1, tiled=True),
        lax.all_gather(values_own, "shard", axis=1, tiled=True),
    )
    keys_all = keys_all.reshape(seqs, full_len, HEADS, head_dim)
    values_all = values_all.reshape(seqs, full_len, HEADS, head_dim)

    def attend(item):
        query_seq, keys_seq, values_seq, doc_rows, doc_cols = item
        scores = (
            jnp.einsum("qhd,khd->hqk", query_seq, keys_seq, preferred_element_type=jnp.float32)
            * scale
        )
        same = (doc_rows[:, None] == doc_cols[None, :])[None]
        masked = jnp.where(same, scores, -1000000000.0)
        top = jnp.max(masked, axis=-1, keepdims=True)
        expo = jnp.exp(masked - top)
        total = jnp.sum(expo, axis=-1, keepdims=True)
        probs_low = (expo / total).astype(jnp.bfloat16)
        mixed_seq = jnp.einsum(
            "hqk,khd->qhd", probs_low, values_seq, preferred_element_type=jnp.float32
        )
        return (mixed_seq.astype(jnp.bfloat16), top + jnp.log(total))

    mixed, logsum = lax.map(attend, (query, keys_all, values_all, doc_own, doc_all))
    mixed_flat = mixed.reshape(seqs * rows, width)
    attended = jnp.dot(mixed_flat, full_out, preferred_element_type=jnp.float32) + full_outb.astype(
        jnp.float32
    )
    first_norm, first_normed, first_scaler = norm_forward(
        flat.astype(jnp.float32) + attended,
        full_g1.astype(jnp.float32),
        full_s1.astype(jnp.float32),
    )
    first_low = first_norm.astype(jnp.bfloat16)
    hidden = jnp.dot(first_low, full_up, preferred_element_type=jnp.float32) + full_upb.astype(
        jnp.float32
    )
    active = jax.nn.gelu(hidden, approximate=False).astype(jnp.bfloat16)
    branch = jnp.dot(active, full_down, preferred_element_type=jnp.float32) + full_downb.astype(
        jnp.float32
    )
    second_out, second_normed, second_scaler = norm_forward(
        first_norm + branch, full_g2.astype(jnp.float32), full_s2.astype(jnp.float32)
    )
    layer_out = second_out.astype(jnp.bfloat16).reshape(seqs, rows, width)
    back_qkv, back_out, back_g1, back_up, back_down, back_g2 = (
        full_qkv,
        full_out,
        full_g1,
        full_up,
        full_down,
        full_g2,
    )
    cotangent = grad_out.reshape(seqs * rows, width).astype(jnp.float32)
    second_gain_grad = jnp.sum(cotangent * second_normed, axis=0)
    second_shift_grad = jnp.sum(cotangent, axis=0)
    grad_second = norm_backward(
        cotangent, second_normed, second_scaler, back_g2.astype(jnp.float32)
    )
    grad_branch = grad_second.astype(jnp.bfloat16)
    down_weight_grad = jnp.einsum(
        "tf,td->fd", active, grad_branch, preferred_element_type=jnp.float32
    )
    down_bias_grad = column_sums(grad_branch)
    grad_active = jnp.einsum(
        "td,fd->tf", grad_branch, back_down, preferred_element_type=jnp.float32
    )
    normal_cdf = 0.5 * (1.0 + lax.erf(hidden * 0.7071067811865476))
    normal_pdf = jnp.exp(-0.5 * hidden * hidden) * 0.3989422804014327
    grad_hidden = (grad_active * (normal_cdf + hidden * normal_pdf)).astype(jnp.bfloat16)
    up_weight_grad = jnp.einsum(
        "td,tf->df", first_low, grad_hidden, preferred_element_type=jnp.float32
    )
    up_bias_grad = column_sums(grad_hidden)
    grad_first_norm = grad_second + jnp.einsum(
        "tf,df->td", grad_hidden, back_up, preferred_element_type=jnp.float32
    )
    first_gain_grad = jnp.sum(grad_first_norm * first_normed, axis=0)
    first_shift_grad = jnp.sum(grad_first_norm, axis=0)
    grad_first = norm_backward(
        grad_first_norm, first_normed, first_scaler, back_g1.astype(jnp.float32)
    )
    grad_attended = grad_first.astype(jnp.bfloat16)
    out_weight_grad = jnp.einsum(
        "td,te->de", mixed_flat, grad_attended, preferred_element_type=jnp.float32
    )
    out_bias_grad = column_sums(grad_attended)
    grad_mixed = jnp.einsum(
        "te,de->td", grad_attended, back_out, preferred_element_type=jnp.float32
    )
    grad_mixed_flat = grad_mixed.astype(jnp.bfloat16).reshape(seqs, rows, width)
    grad_mixed = grad_mixed_flat.reshape(seqs, rows, HEADS, head_dim)

    def attend_back(item):
        query_seq, keys_seq, values_seq, doc_rows, doc_cols, logsum_seq, grad_seq = item
        probs, grad_probs = back_scores(
            query_seq, keys_seq, values_seq, doc_rows, doc_cols, logsum_seq, grad_seq, scale
        )
        probs_low = probs.astype(jnp.bfloat16)
        inner = jnp.sum(probs * grad_probs, axis=-1, keepdims=True)
        grad_scores = (probs * (grad_probs - inner)).astype(jnp.bfloat16)
        grad_query = (
            jnp.einsum("hqk,khd->qhd", grad_scores, keys_seq, preferred_element_type=jnp.float32)
            * scale
        )
        grad_keys = (
            jnp.einsum("hqk,qhd->khd", grad_scores, query_seq, preferred_element_type=jnp.float32)
            * scale
        )
        grad_values = jnp.einsum(
            "hqk,qhd->khd", probs_low, grad_seq, preferred_element_type=jnp.float32
        )
        return (grad_query, grad_keys, grad_values)

    grad_query, grad_keys, grad_values = lax.map(
        attend_back, (query, keys_all, values_all, doc_own, doc_all, logsum, grad_mixed)
    )
    grad_keys = grad_keys.reshape(seqs, full_len, width)
    grad_values = grad_values.reshape(seqs, full_len, width)
    grad_keys, grad_values = (
        lax.psum_scatter(grad_keys, "shard", scatter_dimension=1, tiled=True),
        lax.psum_scatter(grad_values, "shard", scatter_dimension=1, tiled=True),
    )
    grad_qkv = jnp.concatenate(
        [
            grad_query.reshape(seqs * rows, width),
            grad_keys.reshape(seqs * rows, width),
            grad_values.reshape(seqs * rows, width),
        ],
        axis=1,
    ).astype(jnp.bfloat16)
    qkv_weight_grad = jnp.einsum("td,te->de", flat, grad_qkv, preferred_element_type=jnp.float32)
    qkv_sums = column_sums(grad_qkv)
    qv_bias_grad = jnp.concatenate([qkv_sums[:width], qkv_sums[2 * width :]])
    input_grad = grad_first + jnp.einsum(
        "te,de->td", grad_qkv, back_qkv, preferred_element_type=jnp.float32
    )
    input_grad = input_grad.reshape(seqs, rows, width)
    owned = (
        lax.psum_scatter(qkv_weight_grad, "shard", scatter_dimension=0, tiled=True),
        lax.psum_scatter(qv_bias_grad, "shard", scatter_dimension=0, tiled=True),
        lax.psum_scatter(out_weight_grad, "shard", scatter_dimension=0, tiled=True),
        lax.psum_scatter(out_bias_grad, "shard", scatter_dimension=0, tiled=True),
        lax.psum_scatter(first_gain_grad, "shard", scatter_dimension=0, tiled=True),
        lax.psum_scatter(first_shift_grad, "shard", scatter_dimension=0, tiled=True),
        lax.psum_scatter(up_weight_grad, "shard", scatter_dimension=0, tiled=True),
        lax.psum_scatter(up_bias_grad, "shard", scatter_dimension=0, tiled=True),
        lax.psum_scatter(down_weight_grad, "shard", scatter_dimension=0, tiled=True),
        lax.psum_scatter(down_bias_grad, "shard", scatter_dimension=0, tiled=True),
        lax.psum_scatter(second_gain_grad, "shard", scatter_dimension=0, tiled=True),
        lax.psum_scatter(second_shift_grad, "shard", scatter_dimension=0, tiled=True),
    )
    (
        own_qkv,
        own_qv,
        own_out,
        own_outb,
        own_g1,
        own_s1,
        own_up,
        own_upb,
        own_down,
        own_downb,
        own_g2,
        own_s2,
    ) = owned
    banded = (
        lax.psum_scatter(own_qkv, "rep", scatter_dimension=1, tiled=True),
        lax.psum_scatter(own_out, "rep", scatter_dimension=1, tiled=True),
        lax.psum_scatter(own_up, "rep", scatter_dimension=1, tiled=True),
        lax.psum_scatter(own_down, "rep", scatter_dimension=1, tiled=True),
    )
    matrices = (
        lax.all_gather(banded[0], "rep", axis=1, tiled=True),
        lax.all_gather(banded[1], "rep", axis=1, tiled=True),
        lax.all_gather(banded[2], "rep", axis=1, tiled=True),
        lax.all_gather(banded[3], "rep", axis=1, tiled=True),
    )
    smalls = lax.psum((own_qv, own_outb, own_g1, own_s1, own_upb, own_downb, own_g2, own_s2), "rep")
    return (
        layer_out,
        input_grad,
        matrices[0],
        smalls[0],
        matrices[1],
        smalls[1],
        smalls[2],
        smalls[3],
        matrices[2],
        smalls[4],
        matrices[3],
        smalls[5],
        smalls[6],
        smalls[7],
    )


LOW = jnp.bfloat16
FULL = jnp.float32
MESH = pl.DeviceIdType.MESH
BLOCK = 384
CHUNKS = 12
HOPS = 9
VMEM_GRANT = 60 * 1024 * 1024


def greet(partners):
    barrier = pltpu.get_barrier_semaphore()
    for partner in partners:
        pl.semaphore_signal(barrier, inc=1, device_id=partner, device_id_type=MESH)
    pl.semaphore_wait(barrier, len(partners))


def places():
    rep = lax.axis_index("rep")
    y = lax.axis_index("shard")
    core = lax.rem(rep, 2)
    x = lax.rem(rep // 2, 2)
    z0 = lax.rem(rep // 4, 2)
    z1 = rep // 8
    partners = {
        "core": {"rep": rep + 1 - 2 * core},
        "x": {"rep": rep + 2 - 4 * x},
        "z0": {"rep": rep + 4 - 8 * z0},
        "z1": {"rep": rep + 8 - 16 * z1},
        "y": {"shard": 1 - y},
    }
    return core, x, y, z0, z1, partners


def pack_spots(sizes, width):
    spots = []
    start = 0
    for size in sizes:
        spots.append([divmod(start + shift, width) for shift in range(0, size, BLOCK)])
        start += size
    return spots


def gather_kernel(
    x_in, q_in, o_in, u_in, d_in, *rest
):
    count = len(rest) - 9
    vectors, rest = rest[: count // 2], rest[count // 2 :]
    x_out, q_out, o_out, u_out, d_out = rest[:5]
    vector_outs = rest[5 : 5 + count // 2]
    pack, pack_got, send, recv = rest[-4:]
    core, x, y, z0, _, partners = places()
    rows = x_in.shape[1]
    width = x_in.shape[2]
    used = [0]

    def remote(src, dst, way):
        spot = used[0]
        used[0] += 1
        return pltpu.make_async_remote_copy(
            src_ref=src,
            dst_ref=dst,
            send_sem=send.at[spot],
            recv_sem=recv.at[spot],
            device_id=partners[way],
            device_id_type=MESH,
        )

    spots = pack_spots([ref.shape[1] for ref in vectors], pack.shape[1])
    pack[...] = jnp.zeros_like(pack)
    for ref, where in zip(vectors, spots):
        for index, (row, column) in enumerate(where):
            pack[row : row + 1, column : column + BLOCK] = ref[
                :, index * BLOCK : (index + 1) * BLOCK
            ].astype(FULL)

    greet([partners[way] for way in ("y", "x", "z0", "core")])

    pieces = []
    for src, dst in ((q_in, q_out), (o_in, o_out), (u_in, u_out), (d_in, d_out)):
        height = src.shape[0]
        for row in range(0, height, BLOCK):
            for column in range(0, src.shape[1], width):
                pieces.append((src, dst, height, row, pl.ds(column, width)))

    singles = [
        remote(pack, pack_got, "y"),
        remote(x_in.at[1 - y], x_out.at[pl.ds(y * rows, rows)], "y"),
    ]
    for copy in singles:
        copy.start()

    def place(index):
        outer, inner = (x, z0) if index % 2 == 0 else (z0, x)
        return core * 192 + outer * 96, inner * 48

    over_y = []
    for index, (src, dst, height, row, columns) in enumerate(pieces):
        outer, inner = place(index)
        copy = remote(
            src.at[pl.ds(row + outer + inner, 48), columns],
            dst.at[pl.ds(y * height + row + outer + inner, 48), columns],
            "y",
        )
        copy.start()
        over_y.append(copy)

    x_out[pl.ds(pl.multiple_of(y * rows, 16), rows)] = x_in[y]
    for src, dst in ((q_in, q_out), (o_in, o_out), (u_in, u_out), (d_in, d_out)):
        height = src.shape[0]

        def keep(i, carry, src=src, dst=dst, height=height):
            spot = pl.ds(pl.multiple_of(y * height + i * 48, 16), 48)
            dst[spot] = src[pl.ds(pl.multiple_of(i * 48, 16), 48)]
            return carry

        lax.fori_loop(0, height // 48, keep, 0)

    over_first, over_second, over_core = [], [], []
    count = len(pieces)
    for turn in range(count + 2):
        for stage in range(3):
            index = turn - stage
            if index < 0 or index >= count:
                continue
            _, dst, height, row, columns = pieces[index]
            outer, inner = place(index)
            base = (1 - y) * height + row
            if stage == 0:
                over_y[index].wait()
                block = dst.at[pl.ds(base + outer + inner, 48), columns]
                way, made = ("z0" if index % 2 == 0 else "x"), over_first
            elif stage == 1:
                over_first[index].wait()
                block = dst.at[pl.ds(base + outer, 96), columns]
                way, made = ("x" if index % 2 == 0 else "z0"), over_second
            else:
                over_second[index].wait()
                block = dst.at[pl.ds(base + core * 192, 192), columns]
                way, made = "core", over_core
            copy = remote(block, block, way)
            copy.start()
            made.append(copy)
    for copy in singles + over_core:
        copy.wait()
    for ref, where in zip(vector_outs, spots):
        size = ref.shape[1] // 2
        for index, (row, column) in enumerate(where):
            for held, shard in ((pack, y), (pack_got, 1 - y)):
                spot = pl.ds(pl.multiple_of(shard * size + index * BLOCK, 128), BLOCK)
                ref[:, spot] = held[row : row + 1, column : column + BLOCK]


def gather_call(x, q, o, u, d, vectors):
    def doubled(a):
        return jax.ShapeDtypeStruct((2 * a.shape[0],) + a.shape[1:], a.dtype)

    vectors = [v[None, :] for v in vectors]
    longer = [jax.ShapeDtypeStruct((1, 2 * v.shape[1]), FULL) for v in vectors]
    tokens = jax.ShapeDtypeStruct((x.shape[0] * x.shape[1], x.shape[2]), x.dtype)
    inside = pl.BlockSpec(memory_space=pltpu.VMEM)
    return pl.pallas_call(
        gather_kernel,
        out_shape=[tokens, doubled(q), doubled(o), doubled(u), doubled(d)] + longer,
        in_specs=[inside] * (5 + len(vectors)),
        out_specs=[inside] * (5 + len(vectors)),
        scratch_shapes=[
            pltpu.VMEM((8, x.shape[2]), FULL),
            pltpu.VMEM((8, x.shape[2]), FULL),
            pltpu.SemaphoreType.DMA((50,)),
            pltpu.SemaphoreType.DMA((50,)),
        ],
        compiler_params=pltpu.CompilerParams(
            collective_id=0, has_side_effects=True, vmem_limit_bytes=48 * 1024 * 1024
        ),
    )(x, q, o, u, d, *vectors)


def reduce_kernel(
    low1, gh, act, gb, flat, gqkv, mixed, ga, ig, q_sums, v_sums, s2, s3, s4, s5, s6, s7, s8,
    up_out, down_out, qkv_out, out_out, smalls_out, ig_out,
    parts, got_core, got_y, got_x, got_z0, got_z1, whole, small_now, small_sum, small_got,
    send, recv, small_send, small_recv, ig_send, ig_recv, near,
):
    core, x, y, z0, z1, partners = places()
    rows = ig.shape[0] // 2

    greet([partners[way] for way in ("core", "x", "y", "z0", "z1")])

    ig_copy = pltpu.make_async_remote_copy(
        src_ref=ig.at[pl.ds((1 - y) * rows, rows)],
        dst_ref=ig_out,
        send_sem=ig_send,
        recv_sem=ig_recv,
        device_id=partners["y"],
        device_id_type=MESH,
    )
    ig_copy.start()

    row_x = x * 192
    row_z0 = row_x + z0 * 96
    row_z1 = row_z0 + z1 * 48

    def hop(stage, k):
        if stage == 0:
            pair = (parts.at[k, 1 - core], got_core.at[k], "core")
        elif stage == 1:
            pair = (parts.at[k, core, 1 - y], got_y.at[k], "y")
        elif stage == 2:
            pair = (parts.at[k, core, y, pl.ds((1 - x) * 192, 192)], got_x.at[k], "x")
        elif stage == 3:
            pair = (parts.at[k, core, y, pl.ds(row_x + (1 - z0) * 96, 96)], got_z0.at[k], "z0")
        elif stage == 4:
            pair = (parts.at[k, core, y, pl.ds(row_z0 + (1 - z1) * 48, 48)], got_z1.at[k], "z1")
        elif stage == 5:
            block = whole.at[k, core, pl.ds(row_z1, 48)]
            pair = (block, block, "z1")
        elif stage == 6:
            block = whole.at[k, core, pl.ds(row_z0, 96)]
            pair = (block, block, "z0")
        elif stage == 7:
            block = whole.at[k, core, pl.ds(row_x, 192)]
            pair = (block, block, "x")
        else:
            block = whole.at[k, core]
            pair = (block, block, "core")
        return pltpu.make_async_remote_copy(
            src_ref=pair[0],
            dst_ref=pair[1],
            send_sem=send.at[stage, k],
            recv_sem=recv.at[stage, k],
            device_id=partners[pair[2]],
            device_id_type=MESH,
        )

    def product(k, left, left_spots, right, right_spot):
        for half in range(2):
            lhs = left[:, pl.ds(left_spots[half], BLOCK)]
            for side in range(2):
                spot = right_spot + side * BLOCK
                if not isinstance(spot, int):
                    spot = pl.multiple_of(spot, 128)
                rhs = right[:, pl.ds(spot, BLOCK)]
                parts[k, side, half] = lax.dot_general(
                    lhs, rhs, (((0,), (0,)), ((), ())), preferred_element_type=FULL
                ).astype(LOW)

    def store(k, wait):
        def go(out, row, column):
            for side in range(2):
                copy = pltpu.make_async_copy(
                    whole.at[k, side],
                    out.at[pl.ds(row, BLOCK), pl.ds(pl.multiple_of(column + side * BLOCK, 128), BLOCK)],
                    near.at[k, side],
                )
                if wait:
                    copy.wait()
                else:
                    copy.start()

        @pl.when(k < 4)
        def _():
            go(up_out, 0, k * 768)

        @pl.when((k >= 4) & (k < 8))
        def _():
            go(down_out, (k - 4) * BLOCK, 0)

        @pl.when((k >= 8) & (k < 11))
        def _():
            go(qkv_out, 0, (k - 8) * 768)

        @pl.when(k == 11)
        def _():
            go(out_out, 0, 0)

    def compute(k):
        @pl.when(k < 4)
        def _():
            product(k, low1, (0, BLOCK), gh, k * 768)

        @pl.when((k >= 4) & (k < 8))
        def _():
            spot = pl.multiple_of((k - 4) * BLOCK, 128)
            product(k, act, (spot, pl.multiple_of(spot + 4 * BLOCK, 128)), gb, 0)

        @pl.when((k >= 8) & (k < 11))
        def _():
            product(k, flat, (0, BLOCK), gqkv, (k - 8) * 768)

        @pl.when(k == 11)
        def _():
            product(k, mixed, (0, BLOCK), ga, 0)

    def act_on(stage, k):
        if stage == 0:
            compute(k)
        else:
            hop(stage - 1, k).wait()
        if stage == 1:
            for half in range(2):
                parts[k, core, half] = parts[k, core, half] + got_core[k, half]
        elif stage == 2:
            parts[k, core, y] = parts[k, core, y] + got_y[k]
        elif stage == 3:
            spot = pl.ds(pl.multiple_of(row_x, 16), 192)
            parts[k, core, y, spot] = parts[k, core, y, spot] + got_x[k]
        elif stage == 4:
            spot = pl.ds(pl.multiple_of(row_z0, 16), 96)
            parts[k, core, y, spot] = parts[k, core, y, spot] + got_z0[k]
        elif stage == 5:
            spot = pl.ds(pl.multiple_of(row_z1, 16), 48)
            whole[k, core, spot] = parts[k, core, y, spot] + got_z1[k]
        if stage < HOPS:
            hop(stage, k).start()
        else:
            store(k, False)

    small_now[...] = jnp.zeros_like(small_now)
    small_now[0, 0:1] = q_sums[...]
    small_now[1, 0:1] = v_sums[...]
    others = (s2, s3, s4, s5, s6, s7, s8)
    where = pack_spots([768] + [ref.shape[1] // 2 for ref in others], 768)[1:]
    for ref, spots in zip(others, where):
        size = ref.shape[1] // 2
        for half in range(2):
            for index, (row, column) in enumerate(spots):
                shift = half * size + index * BLOCK
                small_now[half, row : row + 1, column : column + BLOCK] = ref[
                    :, shift : shift + BLOCK
                ]
    small_ways = ("core", "y", "x", "z0", "z1")

    def small_hop(stage):
        if stage == 0:
            src, dst = small_now, small_got.at[0]
        elif stage == 1:
            src, dst = small_now.at[1 - y], small_got.at[1, 0]
        else:
            src, dst = small_sum.at[stage - 2], small_got.at[stage, 0]
        return pltpu.make_async_remote_copy(
            src_ref=src,
            dst_ref=dst,
            send_sem=small_send.at[stage],
            recv_sem=small_recv.at[stage],
            device_id=partners[small_ways[stage]],
            device_id_type=MESH,
        )

    def small_step(stage):
        if stage > 0:
            small_hop(stage - 1).wait()
        if stage == 1:
            small_now[...] = small_now[...] + small_got[0]
        elif stage == 2:
            small_sum[0] = small_now[y] + small_got[1, 0]
        elif stage in (3, 4):
            small_sum[stage - 2] = small_sum[stage - 3] + small_got[stage - 1, 0]
        elif stage == 5:
            smalls_out[...] = small_sum[2] + small_got[4, 0]
        if stage < 5:
            small_hop(stage).start()

    def turn(t, carry):
        for stage in range(HOPS + 1):
            @pl.when((t >= stage) & (t < stage + CHUNKS))
            def _(stage=stage):
                act_on(stage, t - stage)

        for stage in range(6):
            @pl.when(t == stage)
            def _(stage=stage):
                small_step(stage)

        return carry

    lax.fori_loop(0, CHUNKS + HOPS, turn, 0)

    def finish(k, carry):
        store(k, True)
        return carry

    lax.fori_loop(0, CHUNKS, finish, 0)
    ig_copy.wait()


def reduce_call(low1, gh, act, gb, flat, gqkv, mixed, ga, smalls, ig):
    packed = (2, 8, flat.shape[1])
    width = flat.shape[1]
    inside = pl.BlockSpec(memory_space=pltpu.VMEM)
    anywhere = pl.BlockSpec(memory_space=pl.ANY)
    half = (ig.shape[0] // 2, width)
    return pl.pallas_call(
        reduce_kernel,
        out_shape=(
            jax.ShapeDtypeStruct((width // 2, gh.shape[1]), LOW),
            jax.ShapeDtypeStruct((act.shape[1] // 2, width), LOW),
            jax.ShapeDtypeStruct((width // 2, gqkv.shape[1]), LOW),
            jax.ShapeDtypeStruct((width // 2, width), LOW),
            jax.ShapeDtypeStruct(packed[1:], FULL),
            jax.ShapeDtypeStruct(half, LOW),
        ),
        in_specs=[inside] * (9 + len(smalls)),
        out_specs=[anywhere] * 4 + [inside, anywhere],
        scratch_shapes=[
            pltpu.VMEM((CHUNKS, 2, 2, BLOCK, BLOCK), LOW),
            pltpu.VMEM((CHUNKS, 2, BLOCK, BLOCK), LOW),
            pltpu.VMEM((CHUNKS, BLOCK, BLOCK), LOW),
            pltpu.VMEM((CHUNKS, 192, BLOCK), LOW),
            pltpu.VMEM((CHUNKS, 96, BLOCK), LOW),
            pltpu.VMEM((CHUNKS, 48, BLOCK), LOW),
            pltpu.VMEM((CHUNKS, 2, BLOCK, BLOCK), LOW),
            pltpu.VMEM(packed, FULL),
            pltpu.VMEM((3,) + packed[1:], FULL),
            pltpu.VMEM((5,) + packed, FULL),
            pltpu.SemaphoreType.DMA((HOPS, CHUNKS)),
            pltpu.SemaphoreType.DMA((HOPS, CHUNKS)),
            pltpu.SemaphoreType.DMA((5,)),
            pltpu.SemaphoreType.DMA((5,)),
            pltpu.SemaphoreType.DMA,
            pltpu.SemaphoreType.DMA,
            pltpu.SemaphoreType.DMA((CHUNKS, 2)),
        ],
        compiler_params=pltpu.CompilerParams(
            collective_id=1, has_side_effects=True, vmem_limit_bytes=VMEM_GRANT
        ),
    )(low1, gh, act, gb, flat, gqkv, mixed, ga, ig, *smalls)


def row_of_sums(values):
    return jnp.sum(values.astype(FULL), axis=0, keepdims=True)


def whole_sequence(
    inputs,
    doc_lengths,
    qkv_weight,
    qv_bias,
    out_weight,
    out_bias,
    first_gain,
    first_shift,
    up_weight,
    up_bias,
    down_weight,
    down_bias,
    second_gain,
    second_shift,
    grad_out,
):
    seqs, rows, width = inputs.shape
    full_len = seqs * rows
    y = lax.axis_index("shard")
    head_dim = width // HEADS
    scale = 1.0 / math.sqrt(head_dim)
    vectors = (
        qv_bias, out_bias, first_gain, first_shift, up_bias, down_bias, second_gain, second_shift
    )
    sizes = [v.shape[0] for v in vectors]
    flat, full_qkv, full_out, full_up, full_down, *whole = gather_call(
        inputs, qkv_weight, out_weight, up_weight, down_weight, vectors
    )
    swap = [(0, 1), (1, 0)]
    grad_other = lax.dynamic_index_in_dim(grad_out, 1 - y, 0, keepdims=False)
    grad_other, flat = lax.optimization_barrier((grad_other, flat))
    grad_other = lax.ppermute(grad_other, "shard", swap)
    grad_own = lax.dynamic_index_in_dim(grad_out, y, 0, keepdims=False)
    cotangent = jnp.concatenate(
        [jnp.where(y == 0, grad_own, grad_other), jnp.where(y == 0, grad_other, grad_own)]
    )
    full_qv, full_outb, full_g1, full_s1, full_upb, full_downb, full_g2, full_s2 = whole
    lengths = lax.dynamic_index_in_dim(doc_lengths, y, 0, keepdims=False)
    ends = jnp.cumsum(lengths)
    spots = jnp.arange(full_len, dtype=jnp.int32)
    docs = jnp.sum((ends[:, None] <= spots[None, :]).astype(jnp.int32), axis=0)
    bias = jnp.concatenate(
        [full_qv[:, :width], jnp.zeros((1, width), FULL), full_qv[:, width:]], axis=1
    )
    qkv = (jnp.dot(flat, full_qkv, preferred_element_type=FULL) + bias).astype(LOW)

    (mixed_flat,) = attend(forward_kernel, qkv, (), docs, scale, head_dim, 1)
    attended = jnp.dot(mixed_flat, full_out, preferred_element_type=FULL) + full_outb
    first_norm, first_normed, first_scaler = norm_forward(
        flat.astype(FULL) + attended, full_g1, full_s1
    )
    first_low = first_norm.astype(LOW)
    hidden = jnp.dot(first_low, full_up, preferred_element_type=FULL) + full_upb
    normal_cdf = 0.5 * (1.0 + lax.erf(hidden * 0.7071067811865476))
    active = (hidden * normal_cdf).astype(LOW)
    branch = jnp.dot(active, full_down, preferred_element_type=FULL) + full_downb
    second_out, second_normed, second_scaler = norm_forward(first_norm + branch, full_g2, full_s2)
    layer_own = second_out.astype(LOW).reshape(seqs, rows, width)
    layer_got = lax.ppermute(
        lax.dynamic_index_in_dim(layer_own, 1 - y, 0, keepdims=False), "shard", swap
    )
    cotangent = cotangent.astype(FULL)
    second_gain_grad = jnp.sum(cotangent * second_normed, axis=0, keepdims=True)
    second_shift_grad = jnp.sum(cotangent, axis=0, keepdims=True)
    grad_second = norm_backward(cotangent, second_normed, second_scaler, full_g2)
    grad_branch = grad_second.astype(LOW)
    down_bias_grad = row_of_sums(grad_branch)
    grad_active = jnp.einsum("td,fd->tf", grad_branch, full_down, preferred_element_type=FULL)
    normal_pdf = jnp.exp(-0.5 * hidden * hidden) * 0.3989422804014327
    grad_hidden = (grad_active * (normal_cdf + hidden * normal_pdf)).astype(LOW)
    up_bias_grad = row_of_sums(grad_hidden)
    grad_first_norm = grad_second + jnp.einsum(
        "tf,df->td", grad_hidden, full_up, preferred_element_type=FULL
    )
    first_gain_grad = jnp.sum(grad_first_norm * first_normed, axis=0, keepdims=True)
    first_shift_grad = jnp.sum(grad_first_norm, axis=0, keepdims=True)
    grad_first = norm_backward(grad_first_norm, first_normed, first_scaler, full_g1)
    grad_attended = grad_first.astype(LOW)
    out_bias_grad = row_of_sums(grad_attended)
    grad_mixed = jnp.einsum(
        "te,de->td", grad_attended, full_out, preferred_element_type=FULL
    ).astype(LOW)
    grad_parts = attend(backward_kernel, qkv, (grad_mixed,), docs, scale, head_dim, 3)
    grad_qkv = jnp.concatenate(grad_parts, axis=1)
    input_grad = grad_first + jnp.einsum(
        "te,de->td", grad_qkv, full_qkv, preferred_element_type=FULL
    )
    small_grads = (
        row_of_sums(grad_parts[0]),
        row_of_sums(grad_parts[2]),
        out_bias_grad,
        first_gain_grad,
        first_shift_grad,
        up_bias_grad,
        down_bias_grad,
        second_gain_grad,
        second_shift_grad,
    )
    up_sum, down_sum, qkv_sum, out_sum, small_sum, grad_got = reduce_call(
        first_low,
        grad_hidden,
        active,
        grad_branch,
        flat,
        grad_qkv,
        mixed_flat,
        grad_attended,
        small_grads,
        input_grad.astype(LOW),
    )
    small_sum = small_sum[:6].reshape(6 * width)
    sums = []
    start = 0
    for size in sizes:
        sums.append(small_sum[start : start + size])
        start += size

    def both(own, got):
        own = lax.dynamic_index_in_dim(own, y, 0, keepdims=False)
        first = jnp.where(y == 0, own, got)
        second = jnp.where(y == 0, got, own)
        return jnp.stack([first, second])

    layer_out = both(layer_own, layer_got)
    input_grad = both(input_grad.reshape(seqs, rows, width), grad_got.astype(FULL))
    return (
        layer_out,
        input_grad,
        qkv_sum.astype(FULL),
        sums[0],
        out_sum.astype(FULL),
        sums[1],
        sums[2],
        sums[3],
        up_sum.astype(FULL),
        sums[4],
        down_sum.astype(FULL),
        sums[5],
        sums[6],
        sums[7],
    )


def pair_probs(query, keys, rows, columns, scale):
    scores = (
        lax.dot_general(query, keys, (((1,), (1,)), ((), ())), preferred_element_type=FULL) * scale
    )
    same = rows == columns
    masked = jnp.where(same, scores, -1000000000.0)
    expo = jnp.exp(masked - jnp.max(masked, axis=-1, keepdims=True))
    return expo / jnp.sum(expo, axis=-1, keepdims=True)


def forward_kernel(scale, head_dim, q_ref, k_ref, v_ref, rows_ref, columns_ref, out_ref):
    for head in range(2):
        spot = pl.ds(head * head_dim, head_dim)
        probs = pair_probs(q_ref[:, spot], k_ref[:, spot], rows_ref[...], columns_ref[...], scale)
        out_ref[:, spot] = jnp.dot(
            probs.astype(LOW), v_ref[:, spot], preferred_element_type=FULL
        ).astype(LOW)


def backward_kernel(
    scale, head_dim, q_ref, k_ref, v_ref, g_ref, rows_ref, columns_ref, gq_ref, gk_ref, gv_ref
):
    for head in range(2):
        spot = pl.ds(head * head_dim, head_dim)
        query, keys, values, grad = q_ref[:, spot], k_ref[:, spot], v_ref[:, spot], g_ref[:, spot]
        probs = pair_probs(query, keys, rows_ref[...], columns_ref[...], scale)
        grad_probs = lax.dot_general(
            grad, values, (((1,), (1,)), ((), ())), preferred_element_type=FULL
        )
        inner = jnp.sum(probs * grad_probs, axis=-1, keepdims=True)
        grad_scores = (probs * (grad_probs - inner)).astype(LOW)
        over_rows = (((0,), (0,)), ((), ()))
        gq_ref[:, spot] = (
            jnp.dot(grad_scores, keys, preferred_element_type=FULL) * scale
        ).astype(LOW)
        gk_ref[:, spot] = (
            lax.dot_general(grad_scores, query, over_rows, preferred_element_type=FULL) * scale
        ).astype(LOW)
        gv_ref[:, spot] = lax.dot_general(
            probs.astype(LOW), grad, over_rows, preferred_element_type=FULL
        ).astype(LOW)


def attend(kernel, qkv, grads, docs, scale, head_dim, outs):
    length = qkv.shape[0]
    width = qkv.shape[1] // 3
    pair = 2 * head_dim
    pairs = width // pair

    def block(third):
        return pl.BlockSpec((length, pair), lambda i: (0, third * pairs + i))

    rows = pl.BlockSpec((length, 1), lambda i: (0, 0))
    columns = pl.BlockSpec((1, length), lambda i: (0, 0))
    return pl.pallas_call(
        functools.partial(kernel, scale, head_dim),
        grid=(pairs,),
        out_shape=[jax.ShapeDtypeStruct((length, width), LOW)] * outs,
        in_specs=[block(0), block(1), block(2)] + [block(0)] * len(grads) + [rows, columns],
        out_specs=[block(0)] * outs,
        compiler_params=pltpu.CompilerParams(vmem_limit_bytes=32 * 1024 * 1024),
    )(qkv, qkv, qkv, *grads, docs[:, None], docs[None, :])


def solution(mesh):
    shape = (mesh.shape["rep"], mesh.shape["shard"])
    return jax.shard_map(
        whole_sequence if shape == (16, 2) else local,
        mesh=mesh,
        in_specs=(
            P("rep", "shard", None),
            P("rep", None),
            P("shard", None),
            P("shard"),
            P("shard", None),
            P("shard"),
            P("shard"),
            P("shard"),
            P("shard", None),
            P("shard"),
            P("shard", None),
            P("shard"),
            P("shard"),
            P("shard"),
            P("rep", "shard", None),
        ),
        out_specs=(
            P("rep", "shard", None),
            P("rep", "shard", None),
            P("shard", None),
            P("shard"),
            P("shard", None),
            P("shard"),
            P("shard"),
            P("shard"),
            P("shard", None),
            P("shard"),
            P("shard", None),
            P("shard"),
            P("shard"),
            P("shard"),
        ),
        check_vma=False,
    )
```
